32 devices in a mesh: pipe: 2 (over core), seq: 16 (over z, y, x).
Axes of the slice: x: 2, y: 2, z: 4, core: 2. Of those that a mesh axis runs over, the one named last changes fastest.
Arguments:
- inputs_saved: bfloat16 [2, 16384, 768], P('pipe', 'seq'), may hold values from -6 to 6
- grad_out: bfloat16 [16384, 768], P('seq'), may hold values from -6 to 6
- value_weight: bfloat16 [2, 768, 768], P('pipe', 'seq'), may hold values from -0.21875 to 0.21875
- gate_weight: bfloat16 [2, 768, 768], P('pipe', 'seq'), may hold values from -0.21875 to 0.21875
- out_weight: bfloat16 [2, 768, 768], P('pipe', 'seq'), may hold values from -0.21875 to 0.21875
- right_factor: bfloat16 [2, 1024, 1024], P('pipe', 'seq'), may hold values from -0.1875 to 0.1875
- left_factor: bfloat16 [2, 16, 16], P('pipe', 'seq'), may hold values from -1.5 to 1.5
- twiddle: float32 [2, 16, 1024], P('pipe', 'seq'), may hold values from -1.5 to 1.5
Outputs:
- input_grads: bfloat16 [2, 16384, 768], P('pipe', 'seq')
The draws below stay inside these ranges and needn't reach their ends.
All inputs are finite; a program needn't handle non-finite values.
Results may differ from the reference program's by a relative error of at most 0.019.
Values may be sent and summed in bfloat16 or wider, within the bound.
No kernel may reach another device: no remote copies, remote signals or barrier semaphores. Data moves between devices by JAX's collectives and lax.ppermute only.
A program may use at most 128 MiB of HBM per device.

```python
import jax
import jax.numpy as jnp

C = 768
B = 1024
A = 16
TOKENS = 16384
LAYERS = 2


def level_of(stream_key, dims, pieces, least, top_value):
    def one(axis_at, parts):
        draws = jax.random.uniform(jax.random.fold_in(jax.random.fold_in(stream_key, 6), axis_at), (parts,), jnp.float32, least / len(pieces), top_value / len(pieces))
        return jnp.repeat(jnp.exp(draws), dims[axis_at] // parts).reshape((-1,) + (1,) * (len(dims) - axis_at - 1))

    gain = one(*pieces[0])
    for cut in pieces[1:]:
        gain = gain * one(*cut)
    return gain


def noise(stream_key, extent, spread, bound, shards=(), kind=jnp.bfloat16):
    loudness = level_of(stream_key, extent, shards, -0.22, 0.18) if shards else 1.0
    drawn = jax.random.normal(stream_key, extent, jnp.float32) * spread * loudness
    return jnp.minimum(jnp.maximum(drawn, -bound), bound).astype(kind)


def setup_inputs(seed: int = 0) -> dict:
    seeds = jax.random.split(jax.random.key(seed), 9)
    return {
        "inputs_saved": noise(seeds[0], (LAYERS, TOKENS, C), 1.0, 6.0, ((0, 2), (1, 16))),
        "grad_out": noise(seeds[1], (TOKENS, C), 1.0, 6.0, ((0, 16),)),
        "value_weight": noise(seeds[2], (LAYERS, C, C), C ** -0.5, 0.21875, ((0, 2), (1, 16))),
        "gate_weight": noise(seeds[3], (LAYERS, C, C), C ** -0.5, 0.21875, ((0, 2), (1, 16))),
        "out_weight": noise(seeds[4], (LAYERS, C, C), C ** -0.5, 0.21875, ((0, 2), (1, 16))),
        "right_factor": noise(seeds[5], (LAYERS, B, B), B ** -0.5, 0.1875, ((0, 2), (1, 16))),
        "left_factor": noise(seeds[6], (LAYERS, A, A), A ** -0.5, 1.5, ((0, 2), (1, 16))),
        "twiddle": jnp.clip(jax.random.uniform(seeds[7], (LAYERS, A, B), jnp.float32, -1.5, 1.5) * level_of(seeds[7], (LAYERS, A, B), ((0, 2), (1, 16)), -0.4, 0.0), -1.5, 1.5),
    }


def layer_grad(saved, incoming, value_weight, gate_weight, out_weight, right_factor, left_factor, twiddle):
    values = jnp.dot(saved, value_weight, preferred_element_type=jnp.float32).astype(jnp.bfloat16)
    gates = jnp.dot(saved, gate_weight, preferred_element_type=jnp.float32).astype(jnp.bfloat16)
    gates_wide = gates.astype(jnp.float32)
    sigma = jax.nn.sigmoid(gates_wide)
    active = gates_wide * sigma
    slope = sigma * (1.0 + gates_wide * (1.0 - sigma))
    mixed = jnp.dot(incoming, out_weight.T, preferred_element_type=jnp.float32).astype(jnp.bfloat16)
    left_part = jnp.dot(left_factor.T, mixed.reshape(A, B * C), preferred_element_type=jnp.float32)
    left_part = left_part.astype(jnp.bfloat16).reshape(A, B, C)
    turned = (left_part.astype(jnp.float32) * twiddle[:, :, None]).astype(jnp.bfloat16)
    right_part = jnp.einsum('pb,apc->abc', right_factor.astype(jnp.float32), turned.astype(jnp.float32))
    right_wide = right_part.astype(jnp.bfloat16).reshape(TOKENS, C).astype(jnp.float32)
    grad_value = (right_wide * active).astype(jnp.bfloat16)
    grad_gate = (right_wide * values.astype(jnp.float32) * slope).astype(jnp.bfloat16)
    total = incoming.astype(jnp.float32)
    total = total + jnp.dot(grad_value, value_weight.T, preferred_element_type=jnp.float32)
    total = total + jnp.dot(grad_gate, gate_weight.T, preferred_element_type=jnp.float32)
    return total.astype(jnp.bfloat16)

def reference(inputs_saved, grad_out, value_weight, gate_weight, out_weight, right_factor, left_factor, twiddle):
    later = layer_grad(inputs_saved[1], grad_out, value_weight[1], gate_weight[1], out_weight[1], right_factor[1], left_factor[1], twiddle[1])
    earlier = layer_grad(inputs_saved[0], later, value_weight[0], gate_weight[0], out_weight[0], right_factor[0], left_factor[0], twiddle[0])
    return jnp.stack([earlier, later])
```

```python
import jax
import jax.numpy as jnp
from jax import lax
from jax.experimental import pallas as pl
from jax.experimental.pallas import tpu as pltpu
from jax.sharding import PartitionSpec as P

BF = jnp.bfloat16
F32 = jnp.float32
SHARDS = 16
ANY = pl.BlockSpec(memory_space=pl.ANY)
VMEM = pl.BlockSpec(memory_space=pltpu.VMEM)
PARAMS = pltpu.CompilerParams(vmem_limit_bytes=48 * 1024 * 1024)

RIGHT, OUT, VALUE, GATE, ROWS = 0, 256, 400, 544, 688


def dot_nn(a, b):
    return lax.dot_general(a, b, (((1,), (0,)), ((), ())), preferred_element_type=F32)


def dot_nt(a, b):
    return lax.dot_general(a, b, (((1,), (1,)), ((), ())), preferred_element_type=F32)


def dot_tn(a, b):
    return lax.dot_general(a, b, (((0,), (0,)), ((), ())), preferred_element_type=F32)


def pack_kernel(right, out, value, gate, blob):
    for g in range(4):
        blob[RIGHT + 64 * g : RIGHT + 64 * g + 64, :] = right[0, :, 256 * g : 256 * g + 256]
    for base, ref in ((OUT, out), (VALUE, value), (GATE, gate)):
        for g in range(3):
            blob[base + 48 * g : base + 48 * g + 48, :] = ref[0, :, 256 * g : 256 * g + 256]


def pack(right, out, value, gate):
    return pl.pallas_call(
        pack_kernel,
        out_shape=jax.ShapeDtypeStruct((ROWS, 256), BF),
        in_specs=[VMEM] * 4,
        out_specs=VMEM,
        name="pack",
    )(right, out, value, gate)


def mix_kernel(section, left, x, y):
    factor = left[SHARDS * section : SHARDS * (section + 1), 0, 0:16].astype(BF)
    rows = lax.broadcasted_iota(jnp.int32, (256, 16), 0)
    cols = lax.broadcasted_iota(jnp.int32, (256, 16), 1)
    spread = jnp.where(rows // 16 == cols, 1.0, 0.0).astype(BF)
    wide = dot_nt(dot_nt(spread, factor).astype(BF), spread)
    at = lax.broadcasted_iota(jnp.int32, (256, 256), 0) % 16
    to = lax.broadcasted_iota(jnp.int32, (256, 256), 1) % 16
    matrix = jnp.where(at == to, wide, 0.0).astype(BF)
    for q in range(2):
        part = x[:, 16 * q : 16 * q + 16, :].reshape(256, x.shape[2])
        y[:, 16 * q : 16 * q + 16, :] = dot_nn(matrix, part).astype(BF).reshape(16, 16, x.shape[2])


def mix(section, left, x):
    x = x.reshape(SHARDS, 32, x.shape[1])
    y = pl.pallas_call(
        lambda *refs: mix_kernel(section, *refs),
        out_shape=jax.ShapeDtypeStruct(x.shape, BF),
        in_specs=[VMEM] * 2,
        out_specs=VMEM,
        name="mix",
        cost_estimate=pl.CostEstimate(flops=2 * 256 * 256 * 768 * 2, bytes_accessed=1600000, transcendentals=0),
    )(left, x)
    return y.reshape(SHARDS * 32, x.shape[2])


def weight_copies(pieces, refs, scratch, sems, first, count):
    seq = lax.axis_index("seq")
    z, place = seq // 4, seq % 4
    copies = []
    for (at, shift, step, offset), ref in zip(pieces, refs):
        del at
        for n, k in enumerate(shift):
            shard = lax.rem(z - k + 4, 4) * 4 + jnp.bitwise_xor(place, step)
            copies.append(
                pltpu.make_async_copy(
                    ref.at[pl.ds(offset + n * ROWS + first, count), :],
                    scratch.at[shard, pl.ds(first, count), :],
                    sems.at[len(copies)],
                )
            )
    assert len(copies) == SHARDS
    return copies


def forward_kernel(pieces, n_refs, *refs):
    x, weights, active, slope, scratch, sems = refs[0], refs[1 : 1 + n_refs], *refs[1 + n_refs :]
    copies = weight_copies(pieces, weights, scratch, sems, VALUE, ROWS - VALUE)
    for c in copies:
        c.start()
    for c in copies:
        c.wait()
    for t in range(2):
        rows = slice(512 * t, 512 * t + 512)
        for e in range(3):
            lanes = slice(256 * e, 256 * e + 256)
            value = scratch[:, VALUE + 48 * e : VALUE + 48 * e + 48, :].reshape(768, 256)
            gate = scratch[:, GATE + 48 * e : GATE + 48 * e + 48, :].reshape(768, 256)
            values = dot_nn(x[0, rows, :], value).astype(BF).astype(F32)
            gates = dot_nn(x[0, rows, :], gate).astype(BF).astype(F32)
            sigma = 1.0 / (1.0 + jnp.exp(-gates))
            active[rows, lanes] = (gates * sigma).astype(BF)
            slope[rows, lanes] = (sigma * (1.0 + gates * (1.0 - sigma)) * values).astype(BF)


def forward(x, pieces, weights):
    shape = jax.ShapeDtypeStruct(x.shape[1:], BF)
    return pl.pallas_call(
        lambda *refs: forward_kernel(pieces, len(weights), *refs),
        out_shape=(shape, shape),
        in_specs=[VMEM] + [ANY] * len(weights),
        out_specs=(VMEM, VMEM),
        scratch_shapes=[pltpu.VMEM((SHARDS, ROWS, 256), BF), pltpu.SemaphoreType.DMA((SHARDS,))],
        compiler_params=PARAMS,
        name="forward",
        cost_estimate=pl.CostEstimate(flops=4 * 1024 * 768 * 768, bytes_accessed=8000000, transcendentals=786432),
    )(x, *weights)


def layer_kernel(pieces, n_refs, last, *refs):
    lo, hi, twiddle, active, slope = refs[:5]
    weights, refs = refs[5 : 5 + n_refs], refs[5 + n_refs :]
    if last:
        got_lo, got_hi, own_lo, own_hi, result = refs[:5]
        refs = refs[5:]
    else:
        given, result_lo, result_hi = refs[:3]
        refs = refs[3:]
    scratch, left, turned, inner, act, slo, base, total, sem_w, sem, sem_out = refs
    pipe = lax.axis_index("pipe")
    halves = (slice(0, 512), slice(512, 1024))

    loads = [pltpu.make_async_copy(r, left.at[h], sem.at[n]) for n, (r, h) in enumerate(zip((lo, hi), halves))]
    copies = weight_copies(pieces, weights, scratch, sem_w, 0, VALUE)
    copies_in = weight_copies(pieces, weights, scratch, sem_w.at[pl.ds(SHARDS, SHARDS)], VALUE, ROWS - VALUE)
    gate_loads = [
        pltpu.make_async_copy(active, act, sem.at[2]),
        pltpu.make_async_copy(slope, slo, sem.at[3]),
    ]
    for c in loads + copies + gate_loads + copies_in:
        c.start()
    if last:

        @pl.when(pipe == 0)
        def _():
            for n, (r, h) in enumerate(zip((got_lo, got_hi), halves)):
                pltpu.make_async_copy(r, base.at[h], sem.at[4 + n]).start()

        @pl.when(pipe != 0)
        def _():
            for n, (r, h) in enumerate(zip((own_lo, own_hi), halves)):
                pltpu.make_async_copy(r, base.at[h], sem.at[4 + n]).start()

        base_loads = [pltpu.make_async_copy(r, base.at[h], sem.at[4 + n]) for n, (r, h) in enumerate(zip((got_lo, got_hi), halves))]
    else:
        base_loads = [pltpu.make_async_copy(given, base, sem.at[4])]
        base_loads[0].start()

    for c in loads:
        c.wait()
    column = jnp.broadcast_to(twiddle[...], (128, 1024)).T
    for c in range(6):
        lanes = slice(128 * c, 128 * c + 128)
        turned[:, lanes] = (left[:, lanes].astype(F32) * column).astype(BF)
    for c in copies:
        c.wait()
    for g in range(4):
        right = scratch[:, RIGHT + 64 * g : RIGHT + 64 * g + 64, :].reshape(1024, 256)
        inner[256 * g : 256 * g + 256, :] = dot_tn(right, turned[...]).astype(BF)
    for c in gate_loads + copies_in + base_loads:
        c.wait()
    stores = []
    for t in range(2):
        rows = slice(512 * t, 512 * t + 512)
        right_part = jnp.zeros((512, 768), F32)
        for e in range(3):
            out = scratch[:, OUT + 48 * e : OUT + 48 * e + 48, :].reshape(768, 256)
            right_part = right_part + dot_nt(inner[rows, 256 * e : 256 * e + 256], out)
        right_part = right_part.astype(BF).astype(F32)
        grad_value = (right_part * act[rows, :].astype(F32)).astype(BF)
        grad_gate = (right_part * slo[rows, :].astype(F32)).astype(BF)
        added = jnp.zeros((512, 768), F32)
        for e in range(3):
            lanes = slice(256 * e, 256 * e + 256)
            value = scratch[:, VALUE + 48 * e : VALUE + 48 * e + 48, :].reshape(768, 256)
            gate = scratch[:, GATE + 48 * e : GATE + 48 * e + 48, :].reshape(768, 256)
            added = added + dot_nt(grad_value[:, lanes], value) + dot_nt(grad_gate[:, lanes], gate)
        if last:
            added = jnp.where(pipe == 0, added, 0.0)
        total[rows, :] = (base[rows, :].astype(F32) + added).astype(BF)
        target = result.at[rows] if last else (result_lo, result_hi)[t]
        stores.append(pltpu.make_async_copy(total.at[rows], target, sem_out.at[t]))
        stores[-1].start()
    for c in stores:
        c.wait()


def layer(lo, hi, twiddle, active, slope, pieces, weights, incoming, last):
    half = jax.ShapeDtypeStruct((512, 768), BF)
    whole = jax.ShapeDtypeStruct((1024, 768), BF)
    big = pltpu.VMEM((1024, 768), BF)
    return pl.pallas_call(
        lambda *refs: layer_kernel(pieces, len(weights), last, *refs),
        out_shape=whole if last else (half, half),
        in_specs=[ANY, ANY, VMEM] + [ANY] * (2 + len(weights) + len(incoming)),
        out_specs=ANY if last else (ANY, ANY),
        scratch_shapes=[pltpu.VMEM((SHARDS, ROWS, 256), BF)]
        + [big] * 7
        + [pltpu.SemaphoreType.DMA((2 * SHARDS,)), pltpu.SemaphoreType.DMA((6,)), pltpu.SemaphoreType.DMA((2,))],
        compiler_params=PARAMS,
        name="layer",
        cost_estimate=pl.CostEstimate(flops=2 * 1024 * 768 * (1024 + 3 * 768), bytes_accessed=14000000, transcendentals=0),
    )(lo, hi, twiddle, active, slope, *weights, *incoming)


def sent(x, section, to):
    pairs = [(section * SHARDS + s, section * SHARDS + to(s)) for s in range(SHARDS)]
    return lax.ppermute(x, ("pipe", "seq"), pairs)


def along_z(x, section, k):
    return sent(x, section, lambda s: ((s // 4 + k) % 4) * 4 + s % 4)


def in_plane(x, section, d):
    return sent(x, section, lambda s: s ^ d)


def exchanged(x):
    return lax.all_to_all(x, "seq", split_axis=0, concat_axis=0, tiled=True)


def tied(*xs):
    return lax.optimization_barrier(xs)


def fast_body(inputs_saved, grad_out, value_weight, gate_weight, out_weight, right_factor, left_factor, twiddle):
    pipe = lax.axis_index("pipe")
    blob = pack(right_factor, out_weight, value_weight, gate_weight)
    row = jnp.pad(left_factor[0].astype(F32), ((0, 7), (0, 112)))
    rows = jnp.broadcast_to(row[None], (32, 8, 128)).reshape(256, 128)
    left = lax.all_to_all(rows, ("pipe", "seq"), split_axis=0, concat_axis=0, tiled=True).reshape(32, 8, 128)

    first_z = [along_z(blob, 1, k) for k in (1, 2, 3)]
    first_own = [in_plane(blob, 1, d) for d in (1, 2, 3)]
    sent_rows = lax.dynamic_slice_in_dim(grad_out, pipe * 512, 512, 0)
    arrived = exchanged(sent_rows)
    mixed = mix(1, left, arrived)
    mixed, *tie = tied(mixed, *first_z, *first_own)
    first_z, first_own = tie[:3], tie[3:]
    rest = jnp.concatenate(first_z)
    first_rest = [in_plane(rest, 1, d) for d in (1, 2, 3)]
    blob_later, _ = tied(blob, mixed)
    second_z = [along_z(blob_later, 0, k) for k in (1, 2, 3)]
    back = exchanged(mixed)
    other = lax.ppermute(back, "pipe", [(0, 1)])
    pieces = [(0, (0,), 0, 0)] + [(0, (k,), 0, 0) for k in (1, 2, 3)]
    pieces += [(0, (0,), d, 0) for d in (1, 2, 3)] + [(0, (1, 2, 3), d, 0) for d in (1, 2, 3)]
    weights = [blob, *first_z, *first_own, *first_rest]
    other, *second_z = tied(other, *second_z)
    column = jnp.concatenate([blob, *second_z])
    second_xy = [in_plane(column, 0, d) for d in (1, 2, 3)]
    active, slope = forward(inputs_saved, pieces, weights)
    g_lo, g_hi = layer(other, back, twiddle[0], active, slope, pieces, weights, [grad_out], False)

    got_lo = lax.ppermute(g_lo, "pipe", [(1, 0)])
    got_hi = lax.ppermute(g_hi, "pipe", [(1, 0)])
    arrived = exchanged(jnp.where(pipe == 0, got_lo, g_hi))
    mixed = mix(0, left, arrived)
    back = exchanged(mixed)
    other = lax.ppermute(back, "pipe", [(1, 0)])
    pieces = [(0, (0, 1, 2, 3), 0, 0)] + [(0, (0, 1, 2, 3), d, 0) for d in (1, 2, 3)]
    weights = [column, *second_xy]
    active, slope = forward(inputs_saved, pieces, weights)
    result = layer(back, other, twiddle[0], active, slope, pieces, weights, [got_lo, got_hi, g_lo, g_hi], True)
    return result[None]


def plain_body(inputs_saved, grad_out, value_weight, gate_weight, out_weight, right_factor, left_factor, twiddle):
    value_full, gate_full, out_full, right_full, left_full = (
        lax.all_gather(w[0], "seq", axis=0, tiled=True)
        for w in (value_weight, gate_weight, out_weight, right_factor, left_factor)
    )
    twiddle_own = twiddle[0]
    saved = inputs_saved[0]
    tokens_dev, width = saved.shape
    order = right_full.shape[0]
    blocks_dev, blocks_all = tokens_dev // order, left_full.shape[0]
    values = jnp.dot(saved, value_full, preferred_element_type=F32).astype(BF)
    gates = jnp.dot(saved, gate_full, preferred_element_type=F32).astype(BF).astype(F32)
    sigma = jax.nn.sigmoid(gates)
    active = gates * sigma
    slope = sigma * (1.0 + gates * (1.0 - sigma)) * values.astype(F32)

    def branch(incoming):
        mixed = jnp.dot(incoming, out_full.T, preferred_element_type=F32).astype(BF)
        mixed = mixed.reshape(blocks_dev, order, width)
        spread = lax.all_to_all(mixed, "seq", split_axis=1, concat_axis=0, tiled=True)
        part = spread.shape[1]
        left_part = jnp.dot(left_full.T, spread.reshape(blocks_all, part * width), preferred_element_type=F32).astype(BF)
        left_part = left_part.reshape(blocks_all, part, width)
        left_part = lax.all_to_all(left_part, "seq", split_axis=0, concat_axis=1, tiled=True)
        turned = (left_part.astype(F32) * twiddle_own[:, :, None]).astype(BF)
        right_part = jnp.einsum("pb,apc->abc", right_full, turned, preferred_element_type=F32).astype(BF)
        right_wide = right_part.reshape(tokens_dev, width).astype(F32)
        grad_value = (right_wide * active).astype(BF)
        grad_gate = (right_wide * slope).astype(BF)
        total = incoming.astype(F32)
        total = total + jnp.dot(grad_value, value_full.T, preferred_element_type=F32)
        total = total + jnp.dot(grad_gate, gate_full.T, preferred_element_type=F32)
        return total.astype(BF)

    first = branch(grad_out)
    second = branch(lax.ppermute(first, "pipe", [(1, 0)]))
    return jnp.where(lax.axis_index("pipe") == 1, first, second)[None]


def solution(mesh):
    fast = mesh.shape["pipe"] == 2 and mesh.shape["seq"] == SHARDS
    whole = P("pipe", "seq", None)
    in_specs = (whole, P("seq", None)) + (whole,) * 6
    return jax.shard_map(
        fast_body if fast else plain_body, mesh=mesh, in_specs=in_specs, out_specs=whole, check_vma=False
    )
```

```python
import jax
import jax.numpy as jnp
from jax import lax
from jax.experimental import pallas as pl
from jax.experimental.pallas import tpu as pltpu
from jax.sharding import PartitionSpec as P

BF = jnp.bfloat16
F32 = jnp.float32
SHARDS = 16
ANY = pl.BlockSpec(memory_space=pl.ANY)
VMEM = pl.BlockSpec(memory_space=pltpu.VMEM)
LIGHT = pl.CostEstimate(flops=1, bytes_accessed=1, transcendentals=0)
PARAMS = pltpu.CompilerParams(vmem_limit_bytes=60 * 1024 * 1024)

RIGHT, OUT, VALUE, GATE, ROWS = 0, 256, 400, 544, 688


def dot_nn(a, b):
    return lax.dot_general(a, b, (((1,), (0,)), ((), ())), preferred_element_type=F32)


def dot_nt(a, b):
    return lax.dot_general(a, b, (((1,), (1,)), ((), ())), preferred_element_type=F32)


def dot_tn(a, b):
    return lax.dot_general(a, b, (((0,), (0,)), ((), ())), preferred_element_type=F32)


def pack_kernel(right, out, value, gate, blob):
    for g in range(4):
        blob[RIGHT + 64 * g : RIGHT + 64 * g + 64, :] = right[0, :, 256 * g : 256 * g + 256]
    for base, ref in ((OUT, out), (VALUE, value), (GATE, gate)):
        for g in range(3):
            blob[base + 48 * g : base + 48 * g + 48, :] = ref[0, :, 256 * g : 256 * g + 256]


def pack(right, out, value, gate):
    return pl.pallas_call(
        pack_kernel,
        out_shape=jax.ShapeDtypeStruct((ROWS, 256), BF),
        in_specs=[VMEM] * 4,
        out_specs=VMEM,
        name="pack",
        cost_estimate=LIGHT,
    )(right, out, value, gate)


def rows_kernel(grad, own, got, out, scratch, sem):
    pipe = lax.axis_index("pipe")
    copy = pltpu.make_async_copy(grad.at[pl.ds(pipe * 512, 512), :], scratch, sem)
    copy.start()
    ours, theirs = (jnp.broadcast_to(r[0].astype(F32), (16, 16)) for r in (own, got))
    low = lax.broadcasted_iota(jnp.int32, (16, 16), 0) < 8
    both = jnp.where(low == (pipe == 1), ours, theirs).astype(BF)
    for j in range(SHARDS):
        out[j, 192:208, :] = jnp.zeros((16, 128), BF)
        out[j, 192:208, 0:16] = both
    copy.wait()
    for j in range(SHARDS):
        for c in range(6):
            out[j, 32 * c : 32 * c + 32, :] = scratch[32 * j : 32 * j + 32, 128 * c : 128 * c + 128]


def rows_to_send(grad, own, got):
    return pl.pallas_call(
        rows_kernel,
        out_shape=jax.ShapeDtypeStruct((SHARDS, 208, 128), BF),
        in_specs=[ANY, VMEM, VMEM],
        out_specs=VMEM,
        scratch_shapes=[pltpu.VMEM((512, 768), BF), pltpu.SemaphoreType.DMA],
        name="rows",
        cost_estimate=LIGHT,
    )(grad, own, got)


def mixing_matrix(factor):
    rows = lax.broadcasted_iota(jnp.int32, (256, 16), 0)
    cols = lax.broadcasted_iota(jnp.int32, (256, 16), 1)
    spread = jnp.where(rows // 16 == cols, 1.0, 0.0).astype(BF)
    wide = dot_nt(dot_nt(spread, factor).astype(BF), spread)
    at = lax.broadcasted_iota(jnp.int32, (256, 256), 0) % 16
    to = lax.broadcasted_iota(jnp.int32, (256, 256), 1) % 16
    return jnp.where(at == to, wide, 0.0).astype(BF)


def first_mix_kernel(x, y):
    matrix = mixing_matrix(x[:, 192, 0:16])
    for q in range(2):
        for c in range(6):
            part = x[:, 32 * c + 16 * q : 32 * c + 16 * q + 16, :].reshape(256, 128)
            y[:, 16 * q : 16 * q + 16, 128 * c : 128 * c + 128] = dot_nn(matrix, part).astype(BF).reshape(16, 16, 128)


def second_mix_kernel(left, x, y):
    matrix = mixing_matrix(left[:, 8, 0:16])
    for q in range(2):
        part = x[:, 16 * q : 16 * q + 16, :].reshape(256, 768)
        y[:, 16 * q : 16 * q + 16, :] = dot_nn(matrix, part).astype(BF).reshape(16, 16, 768)


def first_mix(x):
    return pl.pallas_call(
        first_mix_kernel,
        out_shape=jax.ShapeDtypeStruct((SHARDS, 32, 768), BF),
        in_specs=[VMEM],
        out_specs=VMEM,
        name="mix",
        cost_estimate=LIGHT,
    )(x)


def second_mix(first, x):
    return pl.pallas_call(
        second_mix_kernel,
        grid=(1,),
        out_shape=jax.ShapeDtypeStruct((SHARDS, 32, 768), BF),
        in_specs=[pl.BlockSpec((SHARDS, 16, 128), lambda i: (0, 12, 0)), pl.BlockSpec((SHARDS, 32, 768), lambda i: (0, 0, 0))],
        out_specs=pl.BlockSpec((SHARDS, 32, 768), lambda i: (0, 0, 0)),
        name="mix",
        cost_estimate=LIGHT,
    )(first, x)


def stack_kernel(n, *refs):
    ins, out, sems = refs[:n], refs[n], refs[n + 1]
    copies = [pltpu.make_async_copy(r, out.at[pl.ds(ROWS * i, ROWS), :], sems.at[i]) for i, r in enumerate(ins)]
    for c in copies:
        c.start()
    for c in copies:
        c.wait()


def stacked(*parts):
    n = len(parts)
    return pl.pallas_call(
        lambda *refs: stack_kernel(n, *refs),
        out_shape=jax.ShapeDtypeStruct((ROWS * n, 256), BF),
        in_specs=[ANY] * n,
        out_specs=VMEM,
        scratch_shapes=[pltpu.SemaphoreType.DMA((n,))],
        name="stack",
        cost_estimate=LIGHT,
    )(*parts)


def weight_copies(pieces, refs, scratch, sems, first, count):
    seq = lax.axis_index("seq")
    z, place = seq // 4, seq % 4
    copies = []
    for (at, shift, step, offset), ref in zip(pieces, refs):
        del at
        for n, k in enumerate(shift):
            shard = lax.rem(z - k + 4, 4) * 4 + jnp.bitwise_xor(place, step)
            copies.append(
                pltpu.make_async_copy(
                    ref.at[pl.ds(offset + n * ROWS + first, count), :],
                    scratch.at[shard, pl.ds(first, count), :],
                    sems.at[len(copies)],
                )
            )
    assert len(copies) == SHARDS
    return copies


def forward_work(pieces, n_refs, *refs):
    x, weights, active, slope, scratch, sems = refs[0], refs[1 : 1 + n_refs], *refs[1 + n_refs :]
    copies = weight_copies(pieces, weights, scratch, sems, VALUE, ROWS - VALUE)
    for c in copies:
        c.start()
    for c in copies:
        c.wait()
    for t in range(2):
        rows = slice(512 * t, 512 * t + 512)
        for e in range(3):
            lanes = slice(256 * e, 256 * e + 256)
            value = scratch[:, VALUE + 48 * e : VALUE + 48 * e + 48, :].reshape(768, 256)
            gate = scratch[:, GATE + 48 * e : GATE + 48 * e + 48, :].reshape(768, 256)
            values = dot_nn(x[0, rows, :], value).astype(BF).astype(F32)
            gates = dot_nn(x[0, rows, :], gate).astype(BF).astype(F32)
            sigma = 1.0 / (1.0 + jnp.exp(-gates))
            active[rows, lanes] = (gates * sigma).astype(BF)
            slope[rows, lanes] = (sigma * (1.0 + gates * (1.0 - sigma)) * values).astype(BF)


def forward_kernel(section, pieces, n_refs, *refs):
    @pl.when(lax.axis_index("pipe") == section)
    def _():
        forward_work(pieces, n_refs, *refs)


def forward(section, x, pieces, weights):
    shape = jax.ShapeDtypeStruct(x.shape[1:], BF)
    return pl.pallas_call(
        lambda *refs: forward_kernel(section, pieces, len(weights), *refs),
        out_shape=(shape, shape),
        in_specs=[VMEM] + [ANY] * len(weights),
        out_specs=(VMEM, VMEM),
        scratch_shapes=[pltpu.VMEM((SHARDS, ROWS, 256), BF), pltpu.SemaphoreType.DMA((SHARDS,))],
        compiler_params=PARAMS,
        name="forward",
        cost_estimate=LIGHT,
    )(x, *weights)


def layer_work(pieces, n_refs, last, *refs):
    lo, hi, twiddle, active, slope = refs[:5]
    weights, refs = refs[5 : 5 + n_refs], refs[5 + n_refs :]
    if last:
        got_lo, got_hi, own_lo, own_hi, result = refs[:5]
        refs = refs[5:]
    else:
        given, result_lo, result_hi = refs[:3]
        refs = refs[3:]
    scratch, left, turned, inner, act, slo, base, total, sem_w, sem, sem_out = refs
    halves = (slice(0, 512), slice(512, 1024))

    loads = [pltpu.make_async_copy(r, left.at[h], sem.at[n]) for n, (r, h) in enumerate(zip((lo, hi), halves))]
    copies = weight_copies(pieces, weights, scratch, sem_w, 0, VALUE)
    copies_in = weight_copies(pieces, weights, scratch, sem_w.at[pl.ds(SHARDS, SHARDS)], VALUE, ROWS - VALUE)
    gate_loads = [
        pltpu.make_async_copy(active, act, sem.at[2]),
        pltpu.make_async_copy(slope, slo, sem.at[3]),
    ]
    for c in loads + copies + gate_loads + copies_in:
        c.start()
    if last:
        base_loads = [pltpu.make_async_copy(r, base.at[h], sem.at[4 + n]) for n, (r, h) in enumerate(zip((got_lo, got_hi), halves))]
    else:
        base_loads = [pltpu.make_async_copy(given, base, sem.at[4])]
    for c in base_loads:
        c.start()

    for c in loads:
        c.wait()
    column = jnp.broadcast_to(twiddle[...], (128, 1024)).T
    for c in range(6):
        lanes = slice(128 * c, 128 * c + 128)
        turned[:, lanes] = (left[:, lanes].astype(F32) * column).astype(BF)
    for c in copies:
        c.wait()
    for g in range(4):
        right = scratch[:, RIGHT + 64 * g : RIGHT + 64 * g + 64, :].reshape(1024, 256)
        inner[256 * g : 256 * g + 256, :] = dot_tn(right, turned[...]).astype(BF)
    for c in gate_loads + copies_in + base_loads:
        c.wait()
    stores = []
    for t in range(2):
        rows = slice(512 * t, 512 * t + 512)
        right_part = jnp.zeros((512, 768), F32)
        for e in range(3):
            out = scratch[:, OUT + 48 * e : OUT + 48 * e + 48, :].reshape(768, 256)
            right_part = right_part + dot_nt(inner[rows, 256 * e : 256 * e + 256], out)
        right_part = right_part.astype(BF).astype(F32)
        grad_value = (right_part * act[rows, :].astype(F32)).astype(BF)
        grad_gate = (right_part * slo[rows, :].astype(F32)).astype(BF)
        added = jnp.zeros((512, 768), F32)
        for e in range(3):
            lanes = slice(256 * e, 256 * e + 256)
            value = scratch[:, VALUE + 48 * e : VALUE + 48 * e + 48, :].reshape(768, 256)
            gate = scratch[:, GATE + 48 * e : GATE + 48 * e + 48, :].reshape(768, 256)
            added = added + dot_nt(grad_value[:, lanes], value) + dot_nt(grad_gate[:, lanes], gate)
        total[rows, :] = (base[rows, :].astype(F32) + added).astype(BF)
        target = result.at[rows] if last else (result_lo, result_hi)[t]
        stores.append(pltpu.make_async_copy(total.at[rows], target, sem_out.at[t]))
        stores[-1].start()
    for c in stores:
        c.wait()


def layer_kernel(section, pieces, n_refs, last, *refs):
    pipe = lax.axis_index("pipe")

    @pl.when(pipe == section)
    def _():
        layer_work(pieces, n_refs, last, *refs)

    if last:

        @pl.when(pipe != section)
        def _():
            own, result = refs[5 + n_refs + 2 : 5 + n_refs + 4], refs[5 + n_refs + 4]
            total, sem, sem_out = refs[-4], refs[-2], refs[-1]
            loads = [pltpu.make_async_copy(own[t], total.at[512 * t : 512 * t + 512], sem.at[t]) for t in range(2)]
            stores = [
                pltpu.make_async_copy(total.at[512 * t : 512 * t + 512], result.at[512 * t : 512 * t + 512], sem_out.at[t])
                for t in range(2)
            ]
            for c in loads:
                c.start()
            for load, store in zip(loads, stores):
                load.wait()
                store.start()
            for c in stores:
                c.wait()


def layer(section, lo, hi, twiddle, active, slope, pieces, weights, incoming, last):
    half = jax.ShapeDtypeStruct((512, 768), BF)
    whole = jax.ShapeDtypeStruct((1024, 768), BF)
    big = pltpu.VMEM((1024, 768), BF)
    return pl.pallas_call(
        lambda *refs: layer_kernel(section, pieces, len(weights), last, *refs),
        out_shape=whole if last else (half, half),
        in_specs=[ANY, ANY, VMEM] + [ANY] * (2 + len(weights) + len(incoming)),
        out_specs=ANY if last else (ANY, ANY),
        scratch_shapes=[pltpu.VMEM((SHARDS, ROWS, 256), BF)]
        + [big] * 7
        + [pltpu.SemaphoreType.DMA((2 * SHARDS,)), pltpu.SemaphoreType.DMA((6,)), pltpu.SemaphoreType.DMA((2,))],
        compiler_params=PARAMS,
        name="layer",
        cost_estimate=pl.CostEstimate(flops=2 * 1024 * 768 * (1024 + 3 * 768), bytes_accessed=14000000, transcendentals=0),
    )(lo, hi, twiddle, active, slope, *weights, *incoming)


def sent(x, section, to):
    pairs = [(section * SHARDS + s, section * SHARDS + to(s)) for s in range(SHARDS)]
    return lax.ppermute(x, ("pipe", "seq"), pairs)


def along_z(x, section, k):
    return sent(x, section, lambda s: ((s // 4 + k) % 4) * 4 + s % 4)


def in_plane(x, section, d):
    return sent(x, section, lambda s: s ^ d)


def exchanged(x):
    return lax.all_to_all(x, "seq", split_axis=0, concat_axis=0, tiled=True)


def tied(*xs):
    return lax.optimization_barrier(xs)


LATER = (
    [(0, (0,), 0, 0)]
    + [(0, (k,), 0, 0) for k in (1, 2, 3)]
    + [(0, (0,), d, 0) for d in (1, 2, 3)]
    + [(0, (1, 2, 3), d, 0) for d in (1, 2, 3)]
)
EARLIER = tuple((0, (0, 1, 2, 3), d, 0) for d in range(4))


def apart(f, *args):
    shapes = jax.eval_shape(f, *args)
    return lax.cond(
        lax.axis_index("seq") >= 0,
        f,
        lambda *_: jax.tree.map(lambda x: jnp.zeros(x.shape, x.dtype), shapes),
        *args,
    )


def fast_body(inputs_saved, grad_out, value_weight, gate_weight, out_weight, right_factor, left_factor, twiddle):
    pipe = lax.axis_index("pipe")
    swap = [(0, 1), (1, 0)]
    got_left = lax.ppermute(left_factor, "pipe", swap)
    blob, got_left = tied(pack(right_factor, out_weight, value_weight, gate_weight), got_left)

    along = [along_z(blob, 1, k) for k in (1, 2, 3)]
    own = [in_plane(blob, 1, d) for d in (1, 2, 3)]
    rows = rows_to_send(grad_out, left_factor, got_left)
    rows, rest, *own = tied(rows, stacked(*along), *own)
    plane = [in_plane(rest, 1, d) for d in (1, 2, 3)]
    first, mixed = apart(lambda r: (lambda x: (x, first_mix(x)))(exchanged(r)), rows)
    mixed, later_blob, *plane = tied(mixed, blob, *plane)
    weights = [blob, *along, *own, *plane]
    active, slope = forward(1, inputs_saved, LATER, weights)
    later_along = [along_z(later_blob, 0, k) for k in (1, 2, 3)]
    column = stacked(later_blob, *later_along)
    back, active, slope, column = tied(exchanged(mixed).reshape(512, 768), active, slope, column)
    other, column = tied(lax.ppermute(back, "pipe", [(0, 1)]), column)
    later_plane = [in_plane(column, 0, d) for d in (1, 2, 3)]

    def later_layer(other, back, active, slope, *weights):
        g_lo, g_hi = layer(1, other, back, twiddle[0], active, slope, LATER, weights, [grad_out], False)
        got_lo = lax.ppermute(g_lo, "pipe", [(1, 0)])
        return g_lo, g_hi, got_lo, jnp.where(pipe == 0, got_lo, g_hi).reshape(SHARDS, 32, 768)

    g_lo, g_hi, got_lo, rows = apart(later_layer, other, back, active, slope, *weights)

    mixed = apart(lambda r, f: second_mix(f, exchanged(r)), rows, first)
    mixed, g_hi, *later_plane = tied(mixed, g_hi, *later_plane)
    got_hi = lax.ppermute(g_hi, "pipe", [(1, 0)])
    weights = [column, *later_plane]
    active, slope = forward(0, inputs_saved, EARLIER, weights)
    back, active, slope, got_hi = tied(exchanged(mixed).reshape(512, 768), active, slope, got_hi)
    other = lax.ppermute(back, "pipe", [(1, 0)])
    result = layer(0, back, other, twiddle[0], active, slope, EARLIER, weights, [got_lo, got_hi, g_lo, g_hi], True)
    return result[None]


def plain_body(inputs_saved, grad_out, value_weight, gate_weight, out_weight, right_factor, left_factor, twiddle):
    value_full, gate_full, out_full, right_full, left_full = (
        lax.all_gather(w[0], "seq", axis=0, tiled=True)
        for w in (value_weight, gate_weight, out_weight, right_factor, left_factor)
    )
    twiddle_own = twiddle[0]
    saved = inputs_saved[0]
    tokens_dev, width = saved.shape
    order = right_full.shape[0]
    blocks_dev, blocks_all = tokens_dev // order, left_full.shape[0]
    values = jnp.dot(saved, value_full, preferred_element_type=F32).astype(BF)
    gates = jnp.dot(saved, gate_full, preferred_element_type=F32).astype(BF).astype(F32)
    sigma = jax.nn.sigmoid(gates)
    active = gates * sigma
    slope = sigma * (1.0 + gates * (1.0 - sigma)) * values.astype(F32)

    def branch(incoming):
        mixed = jnp.dot(incoming, out_full.T, preferred_element_type=F32).astype(BF)
        mixed = mixed.reshape(blocks_dev, order, width)
        spread = lax.all_to_all(mixed, "seq", split_axis=1, concat_axis=0, tiled=True)
        part = spread.shape[1]
        left_part = jnp.dot(left_full.T, spread.reshape(blocks_all, part * width), preferred_element_type=F32).astype(BF)
        left_part = left_part.reshape(blocks_all, part, width)
        left_part = lax.all_to_all(left_part, "seq", split_axis=0, concat_axis=1, tiled=True)
        turned = (left_part.astype(F32) * twiddle_own[:, :, None]).astype(BF)
        right_part = jnp.einsum("pb,apc->abc", right_full, turned, preferred_element_type=F32).astype(BF)
        right_wide = right_part.reshape(tokens_dev, width).astype(F32)
        grad_value = (right_wide * active).astype(BF)
        grad_gate = (right_wide * slope).astype(BF)
        total = incoming.astype(F32)
        total = total + jnp.dot(grad_value, value_full.T, preferred_element_type=F32)
        total = total + jnp.dot(grad_gate, gate_full.T, preferred_element_type=F32)
        return total.astype(BF)

    first = branch(grad_out)
    second = branch(lax.ppermute(first, "pipe", [(1, 0)]))
    return jnp.where(lax.axis_index("pipe") == 1, first, second)[None]


def solution(mesh):
    fast = mesh.shape["pipe"] == 2 and mesh.shape["seq"] == SHARDS
    whole = P("pipe", "seq", None)
    in_specs = (whole, P("seq", None)) + (whole,) * 6
    return jax.shard_map(
        fast_body if fast else plain_body, mesh=mesh, in_specs=in_specs, out_specs=whole, check_vma=False
    )
```

```python
import jax
import jax.numpy as jnp
from jax import lax
from jax.experimental import pallas as pl
from jax.experimental.pallas import tpu as pltpu
from jax.sharding import PartitionSpec as P

BF = jnp.bfloat16
F32 = jnp.float32
SHARDS = 16
ANY = pl.BlockSpec(memory_space=pl.ANY)
VMEM = pl.BlockSpec(memory_space=pltpu.VMEM)
LIGHT = pl.CostEstimate(flops=1, bytes_accessed=1, transcendentals=0)
PARAMS = pltpu.CompilerParams(vmem_limit_bytes=62 * 1024 * 1024)

RIGHT, OUT, VALUE, GATE, ROWS = 0, 256, 400, 544, 688


def dot_nn(a, b):
    return lax.dot_general(a, b, (((1,), (0,)), ((), ())), preferred_element_type=F32)


def dot_nt(a, b):
    return lax.dot_general(a, b, (((1,), (1,)), ((), ())), preferred_element_type=F32)


def dot_tn(a, b):
    return lax.dot_general(a, b, (((0,), (0,)), ((), ())), preferred_element_type=F32)


def pack_kernel(right, out, value, gate, blob):
    for g in range(4):
        blob[RIGHT + 64 * g : RIGHT + 64 * g + 64, :] = right[0, :, 256 * g : 256 * g + 256]
    for base, ref in ((OUT, out), (VALUE, value), (GATE, gate)):
        for g in range(3):
            blob[base + 48 * g : base + 48 * g + 48, :] = ref[0, :, 256 * g : 256 * g + 256]


def pack(right, out, value, gate):
    return pl.pallas_call(
        pack_kernel,
        out_shape=jax.ShapeDtypeStruct((ROWS, 256), BF),
        in_specs=[VMEM] * 4,
        out_specs=VMEM,
        name="pack",
        cost_estimate=LIGHT,
    )(right, out, value, gate)


GROUPS = 25


def group_copies(block, out, sems, first, count):
    return [
        pltpu.make_async_copy(
            block.at[pl.ds(first, count), :, :, pl.ds(128 * c, 128)],
            out.at[pl.ds(first, count), pl.ds(4 * c, 4)],
            sems.at[c],
        )
        for c in range(6)
    ]


def factor_group(factor, tail, out, sem):
    tail[...] = jnp.zeros((SHARDS, 16, 128), BF)
    tail[:, :, 0:16] = jnp.broadcast_to(factor[0], (SHARDS, 16, 16))
    return pltpu.make_async_copy(tail, out.at[:, GROUPS - 1], sem)


def rows_kernel(section, source, factor, out, block, tail, sems):
    @pl.when(lax.axis_index("pipe") != section)
    def _():
        loads = [pltpu.make_async_copy(source.at[pl.ds(8 * t, 8)], block.at[pl.ds(8 * t, 8)], sems.at[t]) for t in range(2)]
        for c in loads:
            c.start()
        stores = [factor_group(factor, tail, out, sems.at[2])]
        stores[0].start()
        for t in range(2):
            loads[t].wait()
            copies = group_copies(block, out, sems.at[pl.ds(3 + 6 * t, 6)], 8 * t, 8)
            for c in copies:
                c.start()
            stores += copies
        for c in stores:
            c.wait()


def rows_to_send(section, source, factor):
    return pl.pallas_call(
        lambda *refs: rows_kernel(section, *refs),
        out_shape=jax.ShapeDtypeStruct((SHARDS, GROUPS, 16, 128), BF),
        in_specs=[ANY, VMEM],
        out_specs=ANY,
        scratch_shapes=[pltpu.VMEM((SHARDS, 4, 16, 768), BF), pltpu.VMEM((SHARDS, 16, 128), BF), pltpu.SemaphoreType.DMA((15,))],
        compiler_params=PARAMS,
        name="rows",
        cost_estimate=LIGHT,
    )(source.reshape(SHARDS, 4, 16, 768), factor)


def mix_kernel(left, x, y, matrix):
    @pl.when(pl.program_id(0) == 0)
    def _():
        rows = lax.broadcasted_iota(jnp.int32, (256, 16), 0)
        cols = lax.broadcasted_iota(jnp.int32, (256, 16), 1)
        spread = jnp.where(rows // 16 == cols, 1.0, 0.0).astype(BF)
        wide = dot_nt(dot_nt(spread, left[:, 0, 0, 0:16]).astype(BF), spread)
        at = lax.broadcasted_iota(jnp.int32, (256, 256), 0) % 16
        to = lax.broadcasted_iota(jnp.int32, (256, 256), 1) % 16
        matrix[...] = jnp.where(at == to, wide, 0.0).astype(BF)

    for q in range(4):
        part = jnp.concatenate([x[:, 4 * c + q, :, :].reshape(256, 128) for c in range(2)], axis=1)
        y[:, 16 * q : 16 * q + 16, :] = dot_nn(matrix[...], part).astype(BF).reshape(16, 16, 256)


def mix(x):
    return pl.pallas_call(
        mix_kernel,
        grid=(3,),
        out_shape=jax.ShapeDtypeStruct((SHARDS, 64, 768), BF),
        in_specs=[
            pl.BlockSpec((SHARDS, 1, 16, 128), lambda i: (0, GROUPS - 1, 0, 0)),
            pl.BlockSpec((SHARDS, 8, 16, 128), lambda i: (0, i, 0, 0)),
        ],
        out_specs=pl.BlockSpec((SHARDS, 64, 256), lambda i: (0, 0, i)),
        scratch_shapes=[pltpu.VMEM((256, 256), BF)],
        name="mix",
        cost_estimate=LIGHT,
    )(x, x)


def stack_kernel(section, n, *refs):
    ins, out, scratch, sems = refs[:n], refs[n], refs[n + 1], refs[n + 2]

    @pl.when(lax.axis_index("pipe") == section)
    def _():
        copies = [pltpu.make_async_copy(r, scratch.at[pl.ds(ROWS * i, ROWS), :], sems.at[i]) for i, r in enumerate(ins)]
        stores = [
            pltpu.make_async_copy(scratch.at[pl.ds(ROWS * i, ROWS), :], out.at[pl.ds(ROWS * i, ROWS), :], sems.at[n + i])
            for i in range(n)
        ]
        for c in copies:
            c.start()
        for c, d in zip(copies, stores):
            c.wait()
            d.start()
        for d in stores:
            d.wait()


def stacked(section, *parts):
    n = len(parts)
    return pl.pallas_call(
        lambda *refs: stack_kernel(section, n, *refs),
        out_shape=jax.ShapeDtypeStruct((ROWS * n, 256), BF),
        in_specs=[ANY] * n,
        out_specs=ANY,
        scratch_shapes=[pltpu.VMEM((ROWS * n, 256), BF), pltpu.SemaphoreType.DMA((2 * n,))],
        compiler_params=PARAMS,
        name="stack",
        cost_estimate=LIGHT,
    )(*parts)


def weight_copies(pieces, refs, scratch, sems, first, count):
    seq = lax.axis_index("seq")
    z, place = seq // 4, seq % 4
    copies = []
    for (at, shift, step, offset), ref in zip(pieces, refs):
        del at
        for n, k in enumerate(shift):
            shard = lax.rem(z - k + 4, 4) * 4 + jnp.bitwise_xor(place, step)
            copies.append(
                pltpu.make_async_copy(
                    ref.at[pl.ds(offset + n * ROWS + first, count), :],
                    scratch.at[shard, pl.ds(first, count), :],
                    sems.at[len(copies)],
                )
            )
    assert len(copies) == SHARDS
    return copies


def lanes_of(scratch, base, rows, groups):
    parts = [scratch[:, base + rows * g : base + rows * g + rows, :].reshape(SHARDS * rows, 256) for g in range(groups)]
    return jnp.concatenate(parts, axis=1)


def forward_work(pieces, n_refs, *refs):
    x, twiddle, weights, refs = refs[0], refs[1], refs[2 : 2 + n_refs], refs[2 + n_refs :]
    active, slope, turning, gathered, scratch, rows_in, act, slo, right, sem_w, sem, sem_out = refs
    loads = [pltpu.make_async_copy(x.at[0, pl.ds(512 * t, 512)], rows_in.at[pl.ds(512 * t, 512)], sem.at[t]) for t in range(2)]
    copies = weight_copies(pieces, weights, scratch, sem_w, 0, ROWS)
    for c in loads[:1] + copies + loads[1:]:
        c.start()
    for c in copies:
        c.wait()
    stores = []

    def store(source, target):
        stores.append(pltpu.make_async_copy(source, target, sem_out.at[len(stores)]))
        stores[-1].start()

    store(scratch.at[:, pl.ds(OUT, ROWS - OUT), :], gathered)
    for t in range(2):
        loads[t].wait()
        rows = slice(512 * t, 512 * t + 512)
        for e in range(3):
            lanes = slice(256 * e, 256 * e + 256)
            value = scratch[:, VALUE + 48 * e : VALUE + 48 * e + 48, :].reshape(768, 256)
            gate = scratch[:, GATE + 48 * e : GATE + 48 * e + 48, :].reshape(768, 256)
            values = dot_nn(rows_in[rows, :], value).astype(BF).astype(F32)
            gates = dot_nn(rows_in[rows, :], gate).astype(BF).astype(F32)
            sigma = 0.5 + 0.5 * jnp.tanh(0.5 * gates)
            on = gates * sigma
            act[rows, lanes] = on.astype(BF)
            slo[rows, lanes] = ((sigma + on * (1.0 - sigma)) * values).astype(BF)
            step = 3 * t + e
            if step in (0, 1, 3, 4):
                g = (0, 1, 0, 2, 3)[step]
                part = scratch[:, RIGHT + 64 * g : RIGHT + 64 * g + 64, :].reshape(1024, 256)
                right[256 * g : 256 * g + 256, :] = (part.T.astype(F32) * twiddle[...]).astype(BF)
        store(act.at[rows], active.at[rows])
        store(slo.at[rows], slope.at[rows])
        store(right.at[rows], turning.at[rows])
    for c in stores:
        c.wait()


def forward_kernel(section, pieces, n_refs, *refs):
    @pl.when(lax.axis_index("pipe") == section)
    def _():
        forward_work(pieces, n_refs, *refs)


def forward(section, x, twiddle, pieces, weights):
    shape = jax.ShapeDtypeStruct((1024, 768), BF)
    square = jax.ShapeDtypeStruct((1024, 1024), BF)
    rows = jax.ShapeDtypeStruct((SHARDS, ROWS - OUT, 256), BF)
    big = pltpu.VMEM((1024, 768), BF)
    return pl.pallas_call(
        lambda *refs: forward_kernel(section, pieces, len(weights), *refs),
        out_shape=(shape, shape, square, rows),
        in_specs=[ANY, VMEM] + [ANY] * len(weights),
        out_specs=(ANY,) * 4,
        scratch_shapes=[pltpu.VMEM((SHARDS, ROWS, 256), BF), big, big, big, pltpu.VMEM((1024, 1024), BF)]
        + [pltpu.SemaphoreType.DMA((SHARDS,)), pltpu.SemaphoreType.DMA((2,)), pltpu.SemaphoreType.DMA((7,))],
        compiler_params=PARAMS,
        name="forward",
        cost_estimate=LIGHT,
    )(x, twiddle, *weights)


def layer_work(last, *refs):
    given, active, slope, turning, gathered, incoming = refs[:6]
    if last:
        result, refs = refs[7], refs[8:]
    else:
        factor, result, out, refs = refs[6], refs[7], refs[8], refs[9:]
    weights, left, right, inner, act, slo, base, total, sem, sem_out, *tail = refs
    halves = (slice(0, 512), slice(512, 1024))
    loads = []

    def load(source, target):
        loads.append(pltpu.make_async_copy(source, target, sem.at[len(loads)]))
        loads[-1].start()
        return loads[-1]

    part = load(given, left)
    rights = [load(turning.at[h], right.at[h]) for h in halves]
    part.wait()
    rights[0].wait()
    projections = load(gathered, weights)
    inner[halves[0], :] = dot_nn(right[halves[0], :], left[...]).astype(BF)
    gates = []
    for h in halves:
        gates += [load(active.at[h], act.at[h]), load(slope.at[h], slo.at[h]), load(incoming.at[h], base.at[h])]
    rights[1].wait()
    inner[halves[1], :] = dot_nn(right[halves[1], :], left[...]).astype(BF)
    projections.wait()
    stores = [] if last else [factor_group(factor, tail[0], out, sem_out.at[4])]
    for c in stores:
        c.start()
    for t in range(4):
        rows = slice(256 * t, 256 * t + 256)
        pieces = slice(4 * t, 4 * t + 4)
        right_part = dot_nt(inner[rows, :], lanes_of(weights, 0, 48, 3)).astype(BF).astype(F32)
        if t % 2 == 0:
            for c in gates[3 * (t // 2) : 3 * (t // 2) + 3]:
                c.wait()
        grad_value = (right_part * act[rows, :].astype(F32)).astype(BF)
        grad_gate = (right_part * slo[rows, :].astype(F32)).astype(BF)
        added = dot_nt(grad_value, lanes_of(weights, VALUE - OUT, 48, 3)) + dot_nt(grad_gate, lanes_of(weights, GATE - OUT, 48, 3))
        total[pieces] = (base[rows, :].astype(F32) + added).astype(BF).reshape(4, 4, 16, 768)
        copies = [pltpu.make_async_copy(total.at[pieces], result.at[pieces], sem_out.at[t])]
        if not last:
            copies += group_copies(total, out, sem_out.at[pl.ds(5 + 6 * t, 6)], 4 * t, 4)
        for c in copies:
            c.start()
        stores += copies
    for c in stores:
        c.wait()


def layer_kernel(section, last, *refs):
    pipe = lax.axis_index("pipe")

    @pl.when(pipe == section)
    def _():
        layer_work(last, *refs)

    if last:

        @pl.when(pipe != section)
        def _():
            own, result = refs[6], refs[7]
            total, sem, sem_out = refs[-3:]
            halves = [pl.ds(8 * t, 8) for t in range(2)]
            loads = [pltpu.make_async_copy(own.at[h], total.at[h], sem.at[t]) for t, h in enumerate(halves)]
            stores = [pltpu.make_async_copy(total.at[h], result.at[h], sem_out.at[t]) for t, h in enumerate(halves)]
            for c in loads:
                c.start()
            for load, store in zip(loads, stores):
                load.wait()
                store.start()
            for c in stores:
                c.wait()


def layer(section, left, gated, incoming, other, last):
    whole = jax.ShapeDtypeStruct((SHARDS, 4, 16, 768), BF)
    groups = jax.ShapeDtypeStruct((SHARDS, GROUPS, 16, 128), BF)
    big = pltpu.VMEM((1024, 768), BF)
    return pl.pallas_call(
        lambda *refs: layer_kernel(section, last, *refs),
        out_shape=whole if last else (whole, groups),
        in_specs=[ANY] * (2 + len(gated)) + [ANY if last else VMEM],
        out_specs=ANY if last else (ANY, ANY),
        scratch_shapes=[pltpu.VMEM((SHARDS, ROWS - OUT, 256), BF), big, pltpu.VMEM((1024, 1024), BF)]
        + [big] * 4
        + [pltpu.VMEM((SHARDS, 4, 16, 768), BF), pltpu.SemaphoreType.DMA((10,)), pltpu.SemaphoreType.DMA((29,))]
        + ([] if last else [pltpu.VMEM((SHARDS, 16, 128), BF)]),
        compiler_params=PARAMS,
        name="layer",
        cost_estimate=LIGHT,
    )(left, *gated, incoming, other)


def sent(x, section, to):
    pairs = [(section * SHARDS + s, section * SHARDS + to(s)) for s in range(SHARDS)]
    return lax.ppermute(x, ("pipe", "seq"), pairs)


def along_z(x, section, k):
    return sent(x, section, lambda s: ((s // 4 + k) % 4) * 4 + s % 4)


def in_plane(x, section, d):
    return sent(x, section, lambda s: s ^ d)


def exchanged(x):
    return lax.all_to_all(x, "seq", split_axis=0, concat_axis=0, tiled=True)


def tied(*xs):
    return lax.optimization_barrier(xs)


PIECES = (
    [(0, (0,), 0, 0)]
    + [(0, (k,), 0, 0) for k in (1, 2, 3)]
    + [(0, (0,), d, 0) for d in (1, 2, 3)]
    + [(0, (1, 2, 3), d, 0) for d in (1, 2, 3)]
)


def only_on(core, f, *args):
    shapes, tree = jax.tree.flatten(jax.eval_shape(f, *args))

    def idle(*_):
        arrays = pl.pallas_call(
            lambda *refs: None, out_shape=shapes, out_specs=[ANY] * len(shapes), name="idle", cost_estimate=LIGHT
        )()
        return jax.tree.unflatten(tree, arrays)

    return lax.cond(lax.axis_index("pipe") == core, f, idle, *args)


def mixed(rows):
    return exchanged(mix(exchanged(rows))).reshape(1024, 768)


def fast_body(inputs_saved, grad_out, value_weight, gate_weight, out_weight, right_factor, left_factor, twiddle):
    got_left = lax.ppermute(left_factor, "pipe", [(0, 1), (1, 0)])
    blob, got_left = tied(pack(right_factor, out_weight, value_weight, gate_weight), got_left)

    along = [along_z(blob, 1, k) for k in (1, 2, 3)]
    own = [in_plane(blob, 1, d) for d in (1, 2, 3)]
    rest, *own = tied(stacked(1, *along), *own)
    plane = [in_plane(rest, 1, d) for d in (1, 2, 3)]
    left = only_on(0, mixed, rows_to_send(1, grad_out, got_left))
    left, *plane = tied(left, *plane)
    gated = forward(1, inputs_saved, twiddle[0], PIECES, [blob, *along, *own, *plane])
    left, later_blob, *gated = tied(left, blob, *gated)
    got = lax.ppermute(left, "pipe", [(0, 1)])
    along = [along_z(later_blob, 0, k) for k in (1, 2, 3)]
    own = [in_plane(later_blob, 0, d) for d in (1, 2, 3)]
    grad, rows = layer(1, got, gated, grad_out, got_left, False)
    grad, rows, *moved = tied(grad, rows, *along, *own)
    along, own = moved[:3], moved[3:]

    got_grad = lax.ppermute(grad.reshape(1024, 768), "pipe", [(1, 0)])
    left, later_blob, *moved = tied(only_on(1, mixed, rows), later_blob, *along, *own)
    got = lax.ppermute(left, "pipe", [(1, 0)])

    def gathered(x, twiddle, blob, *moved):
        rest = stacked(0, *moved[:3])
        plane = [in_plane(rest, 0, d) for d in (1, 2, 3)]
        return forward(0, x, twiddle, PIECES, [blob, *moved, *plane])

    gated = only_on(0, gathered, inputs_saved, twiddle[0], later_blob, *moved)
    return layer(0, got, gated, got_grad, grad, True).reshape(1, 1024, 768)


def plain_body(inputs_saved, grad_out, value_weight, gate_weight, out_weight, right_factor, left_factor, twiddle):
    value_full, gate_full, out_full, right_full, left_full = (
        lax.all_gather(w[0], "seq", axis=0, tiled=True)
        for w in (value_weight, gate_weight, out_weight, right_factor, left_factor)
    )
    twiddle_own = twiddle[0]
    saved = inputs_saved[0]
    tokens_dev, width = saved.shape
    order = right_full.shape[0]
    blocks_dev, blocks_all = tokens_dev // order, left_full.shape[0]
    values = jnp.dot(saved, value_full, preferred_element_type=F32).astype(BF)
    gates = jnp.dot(saved, gate_full, preferred_element_type=F32).astype(BF).astype(F32)
    sigma = jax.nn.sigmoid(gates)
    active = gates * sigma
    slope = sigma * (1.0 + gates * (1.0 - sigma)) * values.astype(F32)

    def branch(incoming):
        mixed = jnp.dot(incoming, out_full.T, preferred_element_type=F32).astype(BF)
        mixed = mixed.reshape(blocks_dev, order, width)
        spread = lax.all_to_all(mixed, "seq", split_axis=1, concat_axis=0, tiled=True)
        part = spread.shape[1]
        left_part = jnp.dot(left_full.T, spread.reshape(blocks_all, part * width), preferred_element_type=F32).astype(BF)
        left_part = left_part.reshape(blocks_all, part, width)
        left_part = lax.all_to_all(left_part, "seq", split_axis=0, concat_axis=1, tiled=True)
        turned = (left_part.astype(F32) * twiddle_own[:, :, None]).astype(BF)
        right_part = jnp.einsum("pb,apc->abc", right_full, turned, preferred_element_type=F32).astype(BF)
        right_wide = right_part.reshape(tokens_dev, width).astype(F32)
        grad_value = (right_wide * active).astype(BF)
        grad_gate = (right_wide * slope).astype(BF)
        total = incoming.astype(F32)
        total = total + jnp.dot(grad_value, value_full.T, preferred_element_type=F32)
        total = total + jnp.dot(grad_gate, gate_full.T, preferred_element_type=F32)
        return total.astype(BF)

    first = branch(grad_out)
    second = branch(lax.ppermute(first, "pipe", [(1, 0)]))
    return jnp.where(lax.axis_index("pipe") == 1, first, second)[None]


def solution(mesh):
    fast = mesh.shape["pipe"] == 2 and mesh.shape["seq"] == SHARDS
    whole = P("pipe", "seq", None)
    in_specs = (whole, P("seq", None)) + (whole,) * 6
    return jax.shard_map(
        fast_body if fast else plain_body, mesh=mesh, in_specs=in_specs, out_specs=whole, check_vma=False
    )
```

```python
import jax
import jax.numpy as jnp
from jax import lax
from jax.experimental import pallas as pl
from jax.experimental.pallas import tpu as pltpu
from jax.sharding import PartitionSpec as P

BF = jnp.bfloat16
F32 = jnp.float32
SHARDS = 16
ANY = pl.BlockSpec(memory_space=pl.ANY)
VMEM = pl.BlockSpec(memory_space=pltpu.VMEM)
LIGHT = pl.CostEstimate(flops=1, bytes_accessed=1, transcendentals=0)
PARAMS = pltpu.CompilerParams(vmem_limit_bytes=62 * 1024 * 1024)

RIGHT, OUT, VALUE, GATE, ROWS = 0, 256, 400, 544, 688


def dot_nn(a, b):
    return lax.dot_general(a, b, (((1,), (0,)), ((), ())), preferred_element_type=F32)


def dot_nt(a, b):
    return lax.dot_general(a, b, (((1,), (1,)), ((), ())), preferred_element_type=F32)


def dot_tn(a, b):
    return lax.dot_general(a, b, (((0,), (0,)), ((), ())), preferred_element_type=F32)


def pack_kernel(right, out, value, gate, blob):
    for g in range(4):
        blob[RIGHT + 64 * g : RIGHT + 64 * g + 64, :] = right[0, :, 256 * g : 256 * g + 256]
    for base, ref in ((OUT, out), (VALUE, value), (GATE, gate)):
        for g in range(3):
            blob[base + 48 * g : base + 48 * g + 48, :] = ref[0, :, 256 * g : 256 * g + 256]


def pack(right, out, value, gate):
    return pl.pallas_call(
        pack_kernel,
        out_shape=jax.ShapeDtypeStruct((ROWS, 256), BF),
        in_specs=[VMEM] * 4,
        out_specs=VMEM,
        name="pack",
        cost_estimate=LIGHT,
    )(right, out, value, gate)


GROUPS = 25


def group_copies(block, out, sems, first, count):
    return [
        pltpu.make_async_copy(
            block.at[pl.ds(first, count), :, :, pl.ds(128 * c, 128)],
            out.at[pl.ds(first, count), pl.ds(4 * c, 4)],
            sems.at[c],
        )
        for c in range(6)
    ]


def factor_group(factor, tail, out, sem):
    tail[...] = jnp.zeros((SHARDS, 16, 128), BF)
    tail[:, :, 0:16] = jnp.broadcast_to(factor[0], (SHARDS, 16, 16))
    return pltpu.make_async_copy(tail, out.at[:, GROUPS - 1], sem)


def rows_kernel(section, source, factor, out, block, tail, sems):
    @pl.when(lax.axis_index("pipe") != section)
    def _():
        loads = [pltpu.make_async_copy(source.at[pl.ds(8 * t, 8)], block.at[pl.ds(8 * t, 8)], sems.at[t]) for t in range(2)]
        for c in loads:
            c.start()
        stores = [factor_group(factor, tail, out, sems.at[2])]
        stores[0].start()
        for t in range(2):
            loads[t].wait()
            copies = group_copies(block, out, sems.at[pl.ds(3 + 6 * t, 6)], 8 * t, 8)
            for c in copies:
                c.start()
            stores += copies
        for c in stores:
            c.wait()


def rows_to_send(section, source, factor):
    return pl.pallas_call(
        lambda *refs: rows_kernel(section, *refs),
        out_shape=jax.ShapeDtypeStruct((SHARDS, GROUPS, 16, 128), BF),
        in_specs=[ANY, VMEM],
        out_specs=ANY,
        scratch_shapes=[pltpu.VMEM((SHARDS, 4, 16, 768), BF), pltpu.VMEM((SHARDS, 16, 128), BF), pltpu.SemaphoreType.DMA((15,))],
        compiler_params=PARAMS,
        name="rows",
        cost_estimate=LIGHT,
    )(source.reshape(SHARDS, 4, 16, 768), factor)


def mix_kernel(left, x, y, matrix):
    @pl.when(pl.program_id(0) == 0)
    def _():
        rows = lax.broadcasted_iota(jnp.int32, (256, 16), 0)
        cols = lax.broadcasted_iota(jnp.int32, (256, 16), 1)
        spread = jnp.where(rows // 16 == cols, 1.0, 0.0).astype(BF)
        wide = dot_nt(dot_nt(spread, left[:, 0, 0, 0:16]).astype(BF), spread)
        at = lax.broadcasted_iota(jnp.int32, (256, 256), 0) % 16
        to = lax.broadcasted_iota(jnp.int32, (256, 256), 1) % 16
        matrix[...] = jnp.where(at == to, wide, 0.0).astype(BF)

    for q in range(4):
        part = jnp.concatenate([x[:, 4 * c + q, :, :].reshape(256, 128) for c in range(3)], axis=1)
        y[:, 16 * q : 16 * q + 16, :] = dot_nn(matrix[...], part).astype(BF).reshape(16, 16, 384)


def mix(x):
    return pl.pallas_call(
        mix_kernel,
        grid=(2,),
        out_shape=jax.ShapeDtypeStruct((SHARDS, 64, 768), BF),
        in_specs=[
            pl.BlockSpec((SHARDS, 1, 16, 128), lambda i: (0, GROUPS - 1, 0, 0)),
            pl.BlockSpec((SHARDS, 12, 16, 128), lambda i: (0, i, 0, 0)),
        ],
        out_specs=pl.BlockSpec((SHARDS, 64, 384), lambda i: (0, 0, i)),
        scratch_shapes=[pltpu.VMEM((256, 256), BF)],
        name="mix",
        cost_estimate=LIGHT,
    )(x, x)


def stack_kernel(section, n, *refs):
    ins, out, scratch, sems = refs[:n], refs[n], refs[n + 1], refs[n + 2]

    @pl.when(lax.axis_index("pipe") == section)
    def _():
        copies = [pltpu.make_async_copy(r, scratch.at[pl.ds(ROWS * i, ROWS), :], sems.at[i]) for i, r in enumerate(ins)]
        stores = [
            pltpu.make_async_copy(scratch.at[pl.ds(ROWS * i, ROWS), :], out.at[pl.ds(ROWS * i, ROWS), :], sems.at[n + i])
            for i in range(n)
        ]
        for c in copies:
            c.start()
        for c, d in zip(copies, stores):
            c.wait()
            d.start()
        for d in stores:
            d.wait()


def stacked(section, *parts):
    n = len(parts)
    return pl.pallas_call(
        lambda *refs: stack_kernel(section, n, *refs),
        out_shape=jax.ShapeDtypeStruct((ROWS * n, 256), BF),
        in_specs=[ANY] * n,
        out_specs=ANY,
        scratch_shapes=[pltpu.VMEM((ROWS * n, 256), BF), pltpu.SemaphoreType.DMA((2 * n,))],
        compiler_params=PARAMS,
        name="stack",
        cost_estimate=LIGHT,
    )(*parts)


def weight_copies(pieces, refs, scratch, sems, first, count):
    seq = lax.axis_index("seq")
    z, place = seq // 4, seq % 4
    copies = []
    for (at, shift, step, offset), ref in zip(pieces, refs):
        del at
        for n, k in enumerate(shift):
            shard = lax.rem(z - k + 4, 4) * 4 + jnp.bitwise_xor(place, step)
            copies.append(
                pltpu.make_async_copy(
                    ref.at[pl.ds(offset + n * ROWS + first, count), :],
                    scratch.at[shard, pl.ds(first, count), :],
                    sems.at[len(copies)],
                )
            )
    assert len(copies) == SHARDS
    return copies


def lanes_of(scratch, base, rows, groups):
    parts = [scratch[:, base + rows * g : base + rows * g + rows, :].reshape(SHARDS * rows, 256) for g in range(groups)]
    return jnp.concatenate(parts, axis=1)


def forward_work(pieces, n_refs, *refs):
    x, twiddle, weights, refs = refs[0], refs[1], refs[2 : 2 + n_refs], refs[2 + n_refs :]
    active, slope, turning, gathered, scratch, rows_in, act, slo, right, sem_w, sem, sem_out = refs
    tiles = [slice(256 * t, 256 * t + 256) for t in range(4)]
    loads = [pltpu.make_async_copy(x.at[0, rows], rows_in.at[rows], sem.at[t]) for t, rows in enumerate(tiles)]
    copies = weight_copies(pieces, weights, scratch, sem_w, 0, ROWS)
    for c in loads[:1] + copies + loads[1:]:
        c.start()
    for c in copies:
        c.wait()
    stores = []

    def store(source, target):
        stores.append(pltpu.make_async_copy(source, target, sem_out.at[len(stores)]))
        stores[-1].start()

    store(scratch.at[:, pl.ds(OUT, ROWS - OUT), :], gathered)
    for t, rows in enumerate(tiles):
        loads[t].wait()
        part = scratch[:, RIGHT + 64 * t : RIGHT + 64 * t + 64, :].reshape(1024, 256)
        right[rows, :] = (part.T.astype(F32) * twiddle[...]).astype(BF)
        store(right.at[rows], turning.at[rows])
        for e in range(3):
            lanes = slice(256 * e, 256 * e + 256)
            value = scratch[:, VALUE + 48 * e : VALUE + 48 * e + 48, :].reshape(768, 256)
            gate = scratch[:, GATE + 48 * e : GATE + 48 * e + 48, :].reshape(768, 256)
            values = dot_nn(rows_in[rows, :], value).astype(BF).astype(F32)
            gates = dot_nn(rows_in[rows, :], gate).astype(BF).astype(F32)
            sigma = 0.5 + 0.5 * jnp.tanh(0.5 * gates)
            on = gates * sigma
            act[rows, lanes] = on.astype(BF)
            slo[rows, lanes] = ((sigma + on * (1.0 - sigma)) * values).astype(BF)
        store(act.at[rows], active.at[rows])
        store(slo.at[rows], slope.at[rows])
    for c in stores:
        c.wait()


def forward_kernel(section, pieces, n_refs, *refs):
    @pl.when(lax.axis_index("pipe") == section)
    def _():
        forward_work(pieces, n_refs, *refs)


def forward(section, x, twiddle, pieces, weights):
    shape = jax.ShapeDtypeStruct((1024, 768), BF)
    square = jax.ShapeDtypeStruct((1024, 1024), BF)
    rows = jax.ShapeDtypeStruct((SHARDS, ROWS - OUT, 256), BF)
    big = pltpu.VMEM((1024, 768), BF)
    return pl.pallas_call(
        lambda *refs: forward_kernel(section, pieces, len(weights), *refs),
        out_shape=(shape, shape, square, rows),
        in_specs=[ANY, VMEM] + [ANY] * len(weights),
        out_specs=(ANY,) * 4,
        scratch_shapes=[pltpu.VMEM((SHARDS, ROWS, 256), BF), big, big, big, pltpu.VMEM((1024, 1024), BF)]
        + [pltpu.SemaphoreType.DMA((SHARDS,)), pltpu.SemaphoreType.DMA((4,)), pltpu.SemaphoreType.DMA((13,))],
        compiler_params=PARAMS,
        name="forward",
        cost_estimate=LIGHT,
    )(x, twiddle, *weights)


def layer_work(last, *refs):
    given, active, slope, turning, gathered, incoming = refs[:6]
    if last:
        result, refs = refs[7], refs[8:]
    else:
        factor, result, out, refs = refs[6], refs[7], refs[8], refs[9:]
    weights, left, right, inner, act, slo, base, total, sem, sem_out, *tail = refs
    halves = (slice(0, 512), slice(512, 1024))
    loads = []

    def load(source, target):
        loads.append(pltpu.make_async_copy(source, target, sem.at[len(loads)]))
        loads[-1].start()
        return loads[-1]

    part = load(given, left)
    rights = [load(turning.at[h], right.at[h]) for h in halves]
    part.wait()
    rights[0].wait()
    projections = load(gathered, weights)
    inner[halves[0], :] = dot_nn(right[halves[0], :], left[...]).astype(BF)
    gates = []
    for h in halves:
        gates += [load(active.at[h], act.at[h]), load(slope.at[h], slo.at[h]), load(incoming.at[h], base.at[h])]
    rights[1].wait()
    inner[halves[1], :] = dot_nn(right[halves[1], :], left[...]).astype(BF)
    projections.wait()
    stores = [] if last else [factor_group(factor, tail[0], out, sem_out.at[4])]
    for c in stores:
        c.start()
    for t in range(4):
        rows = slice(256 * t, 256 * t + 256)
        pieces = slice(4 * t, 4 * t + 4)
        right_part = dot_nt(inner[rows, :], lanes_of(weights, 0, 48, 3)).astype(BF).astype(F32)
        if t % 2 == 0:
            for c in gates[3 * (t // 2) : 3 * (t // 2) + 3]:
                c.wait()
        grad_value = (right_part * act[rows, :].astype(F32)).astype(BF)
        grad_gate = (right_part * slo[rows, :].astype(F32)).astype(BF)
        added = dot_nt(grad_value, lanes_of(weights, VALUE - OUT, 48, 3)) + dot_nt(grad_gate, lanes_of(weights, GATE - OUT, 48, 3))
        total[pieces] = (base[rows, :].astype(F32) + added).astype(BF).reshape(4, 4, 16, 768)
        copies = [pltpu.make_async_copy(total.at[pieces], result.at[pieces], sem_out.at[t])]
        if not last:
            copies += group_copies(total, out, sem_out.at[pl.ds(5 + 6 * t, 6)], 4 * t, 4)
        for c in copies:
            c.start()
        stores += copies
    for c in stores:
        c.wait()


def layer_kernel(section, last, *refs):
    pipe = lax.axis_index("pipe")

    @pl.when(pipe == section)
    def _():
        layer_work(last, *refs)

    if last:

        @pl.when(pipe != section)
        def _():
            own, result = refs[6], refs[7]
            total, sem, sem_out = refs[-3:]
            halves = [pl.ds(8 * t, 8) for t in range(2)]
            loads = [pltpu.make_async_copy(own.at[h], total.at[h], sem.at[t]) for t, h in enumerate(halves)]
            stores = [pltpu.make_async_copy(total.at[h], result.at[h], sem_out.at[t]) for t, h in enumerate(halves)]
            for c in loads:
                c.start()
            for load, store in zip(loads, stores):
                load.wait()
                store.start()
            for c in stores:
                c.wait()


def layer(section, left, gated, incoming, other, last):
    whole = jax.ShapeDtypeStruct((SHARDS, 4, 16, 768), BF)
    groups = jax.ShapeDtypeStruct((SHARDS, GROUPS, 16, 128), BF)
    big = pltpu.VMEM((1024, 768), BF)
    return pl.pallas_call(
        lambda *refs: layer_kernel(section, last, *refs),
        out_shape=whole if last else (whole, groups),
        in_specs=[ANY] * (2 + len(gated)) + [ANY if last else VMEM],
        out_specs=ANY if last else (ANY, ANY),
        scratch_shapes=[pltpu.VMEM((SHARDS, ROWS - OUT, 256), BF), big, pltpu.VMEM((1024, 1024), BF)]
        + [big] * 4
        + [pltpu.VMEM((SHARDS, 4, 16, 768), BF), pltpu.SemaphoreType.DMA((10,)), pltpu.SemaphoreType.DMA((29,))]
        + ([] if last else [pltpu.VMEM((SHARDS, 16, 128), BF)]),
        compiler_params=PARAMS,
        name="layer",
        cost_estimate=LIGHT,
    )(left, *gated, incoming, other)


def sent(x, section, to):
    pairs = [(section * SHARDS + s, section * SHARDS + to(s)) for s in range(SHARDS)]
    return lax.ppermute(x, ("pipe", "seq"), pairs)


def along_z(x, section, k):
    return sent(x, section, lambda s: ((s // 4 + k) % 4) * 4 + s % 4)


def in_plane(x, section, d):
    return sent(x, section, lambda s: s ^ d)


def exchanged(x):
    return lax.all_to_all(x, "seq", split_axis=0, concat_axis=0, tiled=True)


def tied(*xs):
    return lax.optimization_barrier(xs)


PIECES = (
    [(0, (0,), 0, 0)]
    + [(0, (k,), 0, 0) for k in (1, 2, 3)]
    + [(0, (0,), d, 0) for d in (1, 2, 3)]
    + [(0, (1, 2, 3), d, 0) for d in (1, 2, 3)]
)


def only_on(core, f, *args):
    shapes, tree = jax.tree.flatten(jax.eval_shape(f, *args))

    def idle(*_):
        arrays = pl.pallas_call(
            lambda *refs: None, out_shape=shapes, out_specs=[ANY] * len(shapes), name="idle", cost_estimate=LIGHT
        )()
        return jax.tree.unflatten(tree, arrays)

    return lax.cond(lax.axis_index("pipe") == core, f, idle, *args)


def mixed(rows):
    return exchanged(mix(exchanged(rows))).reshape(1024, 768)


def fast_body(inputs_saved, grad_out, value_weight, gate_weight, out_weight, right_factor, left_factor, twiddle):
    got_left = lax.ppermute(left_factor, "pipe", [(0, 1), (1, 0)])
    blob, got_left = tied(pack(right_factor, out_weight, value_weight, gate_weight), got_left)

    along = [along_z(blob, 1, k) for k in (1, 2, 3)]
    own = [in_plane(blob, 1, d) for d in (1, 2, 3)]
    rest, *own = tied(stacked(1, *along), *own)
    plane = [in_plane(rest, 1, d) for d in (1, 2, 3)]
    left = only_on(0, mixed, rows_to_send(1, grad_out, got_left))
    left, *plane = tied(left, *plane)
    gated = forward(1, inputs_saved, twiddle[0], PIECES, [blob, *along, *own, *plane])
    left, later_blob, *gated = tied(left, blob, *gated)
    got = lax.ppermute(left, "pipe", [(0, 1)])
    along = [along_z(later_blob, 0, k) for k in (1, 2, 3)]
    own = [in_plane(later_blob, 0, d) for d in (1, 2, 3)]
    grad, rows = layer(1, got, gated, grad_out, got_left, False)
    grad, rows, *moved = tied(grad, rows, *along, *own)
    along, own = moved[:3], moved[3:]

    got_grad = lax.ppermute(grad.reshape(1024, 768), "pipe", [(1, 0)])
    left, later_blob, *moved = tied(only_on(1, mixed, rows), later_blob, *along, *own)
    got = lax.ppermute(left, "pipe", [(1, 0)])

    def gathered(x, twiddle, blob, *moved):
        rest = stacked(0, *moved[:3])
        plane = [in_plane(rest, 0, d) for d in (1, 2, 3)]
        return forward(0, x, twiddle, PIECES, [blob, *moved, *plane])

    gated = only_on(0, gathered, inputs_saved, twiddle[0], later_blob, *moved)
    return layer(0, got, gated, got_grad, grad, True).reshape(1, 1024, 768)


def plain_body(inputs_saved, grad_out, value_weight, gate_weight, out_weight, right_factor, left_factor, twiddle):
    value_full, gate_full, out_full, right_full, left_full = (
        lax.all_gather(w[0], "seq", axis=0, tiled=True)
        for w in (value_weight, gate_weight, out_weight, right_factor, left_factor)
    )
    twiddle_own = twiddle[0]
    saved = inputs_saved[0]
    tokens_dev, width = saved.shape
    order = right_full.shape[0]
    blocks_dev, blocks_all = tokens_dev // order, left_full.shape[0]
    values = jnp.dot(saved, value_full, preferred_element_type=F32).astype(BF)
    gates = jnp.dot(saved, gate_full, preferred_element_type=F32).astype(BF).astype(F32)
    sigma = jax.nn.sigmoid(gates)
    active = gates * sigma
    slope = sigma * (1.0 + gates * (1.0 - sigma)) * values.astype(F32)

    def branch(incoming):
        mixed = jnp.dot(incoming, out_full.T, preferred_element_type=F32).astype(BF)
        mixed = mixed.reshape(blocks_dev, order, width)
        spread = lax.all_to_all(mixed, "seq", split_axis=1, concat_axis=0, tiled=True)
        part = spread.shape[1]
        left_part = jnp.dot(left_full.T, spread.reshape(blocks_all, part * width), preferred_element_type=F32).astype(BF)
        left_part = left_part.reshape(blocks_all, part, width)
        left_part = lax.all_to_all(left_part, "seq", split_axis=0, concat_axis=1, tiled=True)
        turned = (left_part.astype(F32) * twiddle_own[:, :, None]).astype(BF)
        right_part = jnp.einsum("pb,apc->abc", right_full, turned, preferred_element_type=F32).astype(BF)
        right_wide = right_part.reshape(tokens_dev, width).astype(F32)
        grad_value = (right_wide * active).astype(BF)
        grad_gate = (right_wide * slope).astype(BF)
        total = incoming.astype(F32)
        total = total + jnp.dot(grad_value, value_full.T, preferred_element_type=F32)
        total = total + jnp.dot(grad_gate, gate_full.T, preferred_element_type=F32)
        return total.astype(BF)

    first = branch(grad_out)
    second = branch(lax.ppermute(first, "pipe", [(1, 0)]))
    return jnp.where(lax.axis_index("pipe") == 1, first, second)[None]


def solution(mesh):
    fast = mesh.shape["pipe"] == 2 and mesh.shape["seq"] == SHARDS
    whole = P("pipe", "seq", None)
    in_specs = (whole, P("seq", None)) + (whole,) * 6
    return jax.shard_map(
        fast_body if fast else plain_body, mesh=mesh, in_specs=in_specs, out_specs=whole, check_vma=False
    )
```

```python
import jax
import jax.numpy as jnp
from jax import lax
from jax.experimental import pallas as pl
from jax.experimental.pallas import tpu as pltpu
from jax.sharding import PartitionSpec as P

BF = jnp.bfloat16
F32 = jnp.float32
SHARDS = 16
ANY = pl.BlockSpec(memory_space=pl.ANY)
VMEM = pl.BlockSpec(memory_space=pltpu.VMEM)
LIGHT = pl.CostEstimate(flops=1, bytes_accessed=1, transcendentals=0)
PARAMS = pltpu.CompilerParams(vmem_limit_bytes=62 * 1024 * 1024)

RIGHT, OUT, VALUE, GATE, ROWS = 0, 256, 400, 544, 688


def dot_nn(a, b):
    return lax.dot_general(a, b, (((1,), (0,)), ((), ())), preferred_element_type=F32)


def dot_nt(a, b):
    return lax.dot_general(a, b, (((1,), (1,)), ((), ())), preferred_element_type=F32)


def dot_tn(a, b):
    return lax.dot_general(a, b, (((0,), (0,)), ((), ())), preferred_element_type=F32)


def pack_kernel(right, out, value, gate, blob):
    for g in range(4):
        blob[RIGHT + 64 * g : RIGHT + 64 * g + 64, :] = right[0, :, 256 * g : 256 * g + 256]
    for base, ref in ((OUT, out), (VALUE, value), (GATE, gate)):
        for g in range(3):
            blob[base + 48 * g : base + 48 * g + 48, :] = ref[0, :, 256 * g : 256 * g + 256]


def pack(right, out, value, gate):
    return pl.pallas_call(
        pack_kernel,
        out_shape=jax.ShapeDtypeStruct((ROWS, 256), BF),
        in_specs=[VMEM] * 4,
        out_specs=VMEM,
        name="pack",
        cost_estimate=LIGHT,
    )(right, out, value, gate)


GROUPS = 25


def group_copies(block, out, sems, first, count):
    return [
        pltpu.make_async_copy(
            block.at[pl.ds(first, count), :, :, pl.ds(128 * c, 128)],
            out.at[pl.ds(first, count), pl.ds(4 * c, 4)],
            sems.at[c],
        )
        for c in range(6)
    ]


def factor_group(factor, tail, out, sem):
    tail[...] = jnp.zeros((SHARDS, 16, 128), BF)
    tail[:, :, 0:16] = jnp.broadcast_to(factor[0], (SHARDS, 16, 16))
    return pltpu.make_async_copy(tail, out.at[:, GROUPS - 1], sem)


def rows_kernel(section, source, factor, out, block, tail, sems):
    @pl.when(lax.axis_index("pipe") != section)
    def _():
        loads = [pltpu.make_async_copy(source.at[pl.ds(8 * t, 8)], block.at[pl.ds(8 * t, 8)], sems.at[t]) for t in range(2)]
        for c in loads:
            c.start()
        stores = [factor_group(factor, tail, out, sems.at[2])]
        stores[0].start()
        for t in range(2):
            loads[t].wait()
            copies = group_copies(block, out, sems.at[pl.ds(3 + 6 * t, 6)], 8 * t, 8)
            for c in copies:
                c.start()
            stores += copies
        for c in stores:
            c.wait()


def rows_to_send(section, source, factor):
    return pl.pallas_call(
        lambda *refs: rows_kernel(section, *refs),
        out_shape=jax.ShapeDtypeStruct((SHARDS, GROUPS, 16, 128), BF),
        in_specs=[ANY, VMEM],
        out_specs=ANY,
        scratch_shapes=[pltpu.VMEM((SHARDS, 4, 16, 768), BF), pltpu.VMEM((SHARDS, 16, 128), BF), pltpu.SemaphoreType.DMA((15,))],
        compiler_params=PARAMS,
        name="rows",
        cost_estimate=LIGHT,
    )(source.reshape(SHARDS, 4, 16, 768), factor)


def mix_kernel(left, x, y, matrix):
    @pl.when(pl.program_id(0) == 0)
    def _():
        rows = lax.broadcasted_iota(jnp.int32, (256, 16), 0)
        cols = lax.broadcasted_iota(jnp.int32, (256, 16), 1)
        spread = jnp.where(rows // 16 == cols, 1.0, 0.0).astype(BF)
        wide = dot_nt(dot_nt(spread, left[:, 0, 0, 0:16]).astype(BF), spread)
        at = lax.broadcasted_iota(jnp.int32, (256, 256), 0) % 16
        to = lax.broadcasted_iota(jnp.int32, (256, 256), 1) % 16
        matrix[...] = jnp.where(at == to, wide, 0.0).astype(BF)

    for q in range(4):
        part = jnp.concatenate([x[:, 4 * c + q, :, :].reshape(256, 128) for c in range(3)], axis=1)
        y[:, 16 * q : 16 * q + 16, :] = dot_nn(matrix[...], part).astype(BF).reshape(16, 16, 384)


def mix(x):
    return pl.pallas_call(
        mix_kernel,
        grid=(2,),
        out_shape=jax.ShapeDtypeStruct((SHARDS, 64, 768), BF),
        in_specs=[
            pl.BlockSpec((SHARDS, 1, 16, 128), lambda i: (0, GROUPS - 1, 0, 0)),
            pl.BlockSpec((SHARDS, 12, 16, 128), lambda i: (0, i, 0, 0)),
        ],
        out_specs=pl.BlockSpec((SHARDS, 64, 384), lambda i: (0, 0, i)),
        scratch_shapes=[pltpu.VMEM((256, 256), BF)],
        name="mix",
        cost_estimate=LIGHT,
    )(x, x)


def stack_kernel(section, n, *refs):
    ins, out, scratch, sems = refs[:n], refs[n], refs[n + 1], refs[n + 2]

    @pl.when(lax.axis_index("pipe") == section)
    def _():
        copies = [pltpu.make_async_copy(r, scratch.at[pl.ds(ROWS * i, ROWS), :], sems.at[i]) for i, r in enumerate(ins)]
        stores = [
            pltpu.make_async_copy(scratch.at[pl.ds(ROWS * i, ROWS), :], out.at[pl.ds(ROWS * i, ROWS), :], sems.at[n + i])
            for i in range(n)
        ]
        for c in copies:
            c.start()
        for c, d in zip(copies, stores):
            c.wait()
            d.start()
        for d in stores:
            d.wait()


def stacked(section, *parts):
    n = len(parts)
    return pl.pallas_call(
        lambda *refs: stack_kernel(section, n, *refs),
        out_shape=jax.ShapeDtypeStruct((ROWS * n, 256), BF),
        in_specs=[ANY] * n,
        out_specs=ANY,
        scratch_shapes=[pltpu.VMEM((ROWS * n, 256), BF), pltpu.SemaphoreType.DMA((2 * n,))],
        compiler_params=PARAMS,
        name="stack",
        cost_estimate=LIGHT,
    )(*parts)


def weight_copies(pieces, refs, scratch, sems, first, count):
    seq = lax.axis_index("seq")
    z, place = seq // 4, seq % 4
    copies = []
    for (at, shift, step, offset), ref in zip(pieces, refs):
        del at
        for n, k in enumerate(shift):
            shard = lax.rem(z - k + 4, 4) * 4 + jnp.bitwise_xor(place, step)
            copies.append(
                pltpu.make_async_copy(
                    ref.at[pl.ds(offset + n * ROWS + first, count), :],
                    scratch.at[shard, pl.ds(first, count), :],
                    sems.at[len(copies)],
                )
            )
    assert len(copies) == SHARDS
    return copies


def lanes_of(scratch, base, rows, groups):
    parts = [scratch[:, base + rows * g : base + rows * g + rows, :].reshape(SHARDS * rows, 256) for g in range(groups)]
    return jnp.concatenate(parts, axis=1)


def forward_work(pieces, n_refs, *refs):
    x, twiddle, weights, refs = refs[0], refs[1], refs[2 : 2 + n_refs], refs[2 + n_refs :]
    active, slope, turning, gathered, scratch, rows_in, act, slo, right, sem_w, sem, sem_out = refs
    tiles = [slice(256 * t, 256 * t + 256) for t in range(4)]
    loads = [pltpu.make_async_copy(x.at[0, rows], rows_in.at[rows], sem.at[t]) for t, rows in enumerate(tiles)]
    copies = weight_copies(pieces, weights, scratch, sem_w, 0, ROWS)
    for c in loads[:1] + copies + loads[1:]:
        c.start()
    for c in copies:
        c.wait()
    stores = []

    def store(source, target):
        stores.append(pltpu.make_async_copy(source, target, sem_out.at[len(stores)]))
        stores[-1].start()

    store(scratch.at[:, pl.ds(OUT, ROWS - OUT), :], gathered)
    for t, rows in enumerate(tiles):
        loads[t].wait()
        part = scratch[:, RIGHT + 64 * t : RIGHT + 64 * t + 64, :].reshape(1024, 256)
        right[rows, :] = (part.T.astype(F32) * twiddle[...]).astype(BF)
        store(right.at[rows], turning.at[rows])
        for e in range(3):
            lanes = slice(256 * e, 256 * e + 256)
            value = scratch[:, VALUE + 48 * e : VALUE + 48 * e + 48, :].reshape(768, 256)
            gate = scratch[:, GATE + 48 * e : GATE + 48 * e + 48, :].reshape(768, 256)
            values = dot_nn(rows_in[rows, :], value).astype(BF).astype(F32)
            gates = dot_nn(rows_in[rows, :], gate).astype(BF).astype(F32)
            sigma = 0.5 + 0.5 * jnp.tanh(0.5 * gates)
            on = gates * sigma
            act[rows, lanes] = on.astype(BF)
            slo[rows, lanes] = ((sigma + on * (1.0 - sigma)) * values).astype(BF)
        store(act.at[rows], active.at[rows])
        store(slo.at[rows], slope.at[rows])
    for c in stores:
        c.wait()


def forward_kernel(section, pieces, n_refs, *refs):
    @pl.when(lax.axis_index("pipe") == section)
    def _():
        forward_work(pieces, n_refs, *refs)


def forward(section, x, twiddle, pieces, weights):
    shape = jax.ShapeDtypeStruct((1024, 768), BF)
    square = jax.ShapeDtypeStruct((1024, 1024), BF)
    rows = jax.ShapeDtypeStruct((SHARDS, ROWS - OUT, 256), BF)
    big = pltpu.VMEM((1024, 768), BF)
    return pl.pallas_call(
        lambda *refs: forward_kernel(section, pieces, len(weights), *refs),
        out_shape=(shape, shape, square, rows),
        in_specs=[ANY, VMEM] + [ANY] * len(weights),
        out_specs=(ANY,) * 4,
        scratch_shapes=[pltpu.VMEM((SHARDS, ROWS, 256), BF), big, big, big, pltpu.VMEM((1024, 1024), BF)]
        + [pltpu.SemaphoreType.DMA((SHARDS,)), pltpu.SemaphoreType.DMA((4,)), pltpu.SemaphoreType.DMA((13,))],
        compiler_params=PARAMS,
        name="forward",
        cost_estimate=LIGHT,
    )(x, twiddle, *weights)


def layer_work(last, *refs):
    given, active, slope, turning, gathered, incoming = refs[:6]
    if last:
        result, refs = refs[7], refs[8:]
    else:
        factor, result, out, refs = refs[6], refs[7], refs[8], refs[9:]
    weights, left, right, inner, act, slo, base, total, sem, sem_out, *tail = refs
    halves = (slice(0, 512), slice(512, 1024))
    loads = []

    def load(source, target):
        loads.append(pltpu.make_async_copy(source, target, sem.at[len(loads)]))
        loads[-1].start()
        return loads[-1]

    part = load(given, left)
    rights = [load(turning.at[h], right.at[h]) for h in halves]
    part.wait()
    rights[0].wait()
    projections = load(gathered, weights)
    inner[halves[0], :] = dot_nn(right[halves[0], :], left[...]).astype(BF)
    gates = []
    for h in halves:
        gates += [load(active.at[h], act.at[h]), load(slope.at[h], slo.at[h]), load(incoming.at[h], base.at[h])]
    rights[1].wait()
    inner[halves[1], :] = dot_nn(right[halves[1], :], left[...]).astype(BF)
    projections.wait()
    stores = [] if last else [factor_group(factor, tail[0], out, sem_out.at[4])]
    for c in stores:
        c.start()
    for t in range(4):
        rows = slice(256 * t, 256 * t + 256)
        pieces = slice(4 * t, 4 * t + 4)
        right_part = dot_nt(inner[rows, :], lanes_of(weights, 0, 48, 3)).astype(BF).astype(F32)
        if t % 2 == 0:
            for c in gates[3 * (t // 2) : 3 * (t // 2) + 3]:
                c.wait()
        grad_value = (right_part * act[rows, :].astype(F32)).astype(BF)
        grad_gate = (right_part * slo[rows, :].astype(F32)).astype(BF)
        added = dot_nt(grad_value, lanes_of(weights, VALUE - OUT, 48, 3)) + dot_nt(grad_gate, lanes_of(weights, GATE - OUT, 48, 3))
        total[pieces] = (base[rows, :].astype(F32) + added).astype(BF).reshape(4, 4, 16, 768)
        copies = [pltpu.make_async_copy(total.at[pieces], result.at[pieces], sem_out.at[t])]
        if not last:
            copies += group_copies(total, out, sem_out.at[pl.ds(5 + 6 * t, 6)], 4 * t, 4)
        for c in copies:
            c.start()
        stores += copies
    for c in stores:
        c.wait()


def layer_kernel(section, last, *refs):
    pipe = lax.axis_index("pipe")

    @pl.when(pipe == section)
    def _():
        layer_work(last, *refs)

    if last:

        @pl.when(pipe != section)
        def _():
            own, result = refs[6], refs[7]
            total, sem, sem_out = refs[-3:]
            halves = [pl.ds(8 * t, 8) for t in range(2)]
            loads = [pltpu.make_async_copy(own.at[h], total.at[h], sem.at[t]) for t, h in enumerate(halves)]
            stores = [pltpu.make_async_copy(total.at[h], result.at[h], sem_out.at[t]) for t, h in enumerate(halves)]
            for c in loads:
                c.start()
            for load, store in zip(loads, stores):
                load.wait()
                store.start()
            for c in stores:
                c.wait()


def layer(section, left, gated, incoming, other, last):
    whole = jax.ShapeDtypeStruct((SHARDS, 4, 16, 768), BF)
    groups = jax.ShapeDtypeStruct((SHARDS, GROUPS, 16, 128), BF)
    big = pltpu.VMEM((1024, 768), BF)
    return pl.pallas_call(
        lambda *refs: layer_kernel(section, last, *refs),
        out_shape=whole if last else (whole, groups),
        in_specs=[ANY] * (2 + len(gated)) + [ANY if last else VMEM],
        out_specs=ANY if last else (ANY, ANY),
        scratch_shapes=[pltpu.VMEM((SHARDS, ROWS - OUT, 256), BF), big, pltpu.VMEM((1024, 1024), BF)]
        + [big] * 4
        + [pltpu.VMEM((SHARDS, 4, 16, 768), BF), pltpu.SemaphoreType.DMA((10,)), pltpu.SemaphoreType.DMA((29,))]
        + ([] if last else [pltpu.VMEM((SHARDS, 16, 128), BF)]),
        compiler_params=PARAMS,
        name="layer",
        cost_estimate=LIGHT,
    )(left, *gated, incoming, other)


def sent(x, section, to):
    pairs = [(section * SHARDS + s, section * SHARDS + to(s)) for s in range(SHARDS)]
    return lax.ppermute(x, ("pipe", "seq"), pairs)


def along_z(x, section, k):
    return sent(x, section, lambda s: ((s // 4 + k) % 4) * 4 + s % 4)


def in_plane(x, section, d):
    return sent(x, section, lambda s: s ^ d)


def exchanged(x):
    return lax.all_to_all(x, "seq", split_axis=0, concat_axis=0, tiled=True)


def tied(*xs):
    return lax.optimization_barrier(xs)


PIECES = (
    [(0, (0,), 0, 0)]
    + [(0, (k,), 0, 0) for k in (1, 2, 3)]
    + [(0, (0,), d, 0) for d in (3, 1, 2)]
    + [(0, (1, 2, 3), d, 0) for d in (3, 1, 2)]
)


def only_on(core, f, *args):
    shapes, tree = jax.tree.flatten(jax.eval_shape(f, *args))

    def idle(*_):
        arrays = pl.pallas_call(
            lambda *refs: None, out_shape=shapes, out_specs=[ANY] * len(shapes), name="idle", cost_estimate=LIGHT
        )()
        return jax.tree.unflatten(tree, arrays)

    return lax.cond(lax.axis_index("pipe") == core, f, idle, *args)


def mixed(rows):
    return exchanged(mix(exchanged(rows))).reshape(1024, 768)


def fast_body(inputs_saved, grad_out, value_weight, gate_weight, out_weight, right_factor, left_factor, twiddle):
    got_left = lax.ppermute(left_factor, "pipe", [(0, 1), (1, 0)])
    blob, got_left = tied(pack(right_factor, out_weight, value_weight, gate_weight), got_left)

    along = [along_z(blob, 1, k) for k in (1, 2, 3)]
    own = [in_plane(blob, 1, d) for d in (3, 1, 2)]
    rest, *own = tied(stacked(1, *along), *own)
    plane = [in_plane(rest, 1, d) for d in (3, 1, 2)]
    left = only_on(0, mixed, rows_to_send(1, grad_out, got_left))
    left, *plane = tied(left, *plane)
    gated = forward(1, inputs_saved, twiddle[0], PIECES, [blob, *along, *own, *plane])
    left, later_blob, *gated = tied(left, blob, *gated)
    got = lax.ppermute(left, "pipe", [(0, 1)])
    along = [along_z(later_blob, 0, k) for k in (1, 2, 3)]
    own = [in_plane(later_blob, 0, d) for d in (3, 1, 2)]
    grad, rows = layer(1, got, gated, grad_out, got_left, False)
    grad, rows, *moved = tied(grad, rows, *along, *own)
    along, own = moved[:3], moved[3:]

    got_grad = lax.ppermute(grad.reshape(1024, 768), "pipe", [(1, 0)])
    left, later_blob, *moved = tied(only_on(1, mixed, rows), later_blob, *along, *own)
    got = lax.ppermute(left, "pipe", [(1, 0)])

    def gathered(x, twiddle, blob, *moved):
        rest = stacked(0, *moved[:3])
        plane = [in_plane(rest, 0, d) for d in (3, 1, 2)]
        return forward(0, x, twiddle, PIECES, [blob, *moved, *plane])

    gated = only_on(0, gathered, inputs_saved, twiddle[0], later_blob, *moved)
    return layer(0, got, gated, got_grad, grad, True).reshape(1, 1024, 768)


def plain_body(inputs_saved, grad_out, value_weight, gate_weight, out_weight, right_factor, left_factor, twiddle):
    value_full, gate_full, out_full, right_full, left_full = (
        lax.all_gather(w[0], "seq", axis=0, tiled=True)
        for w in (value_weight, gate_weight, out_weight, right_factor, left_factor)
    )
    twiddle_own = twiddle[0]
    saved = inputs_saved[0]
    tokens_dev, width = saved.shape
    order = right_full.shape[0]
    blocks_dev, blocks_all = tokens_dev // order, left_full.shape[0]
    values = jnp.dot(saved, value_full, preferred_element_type=F32).astype(BF)
    gates = jnp.dot(saved, gate_full, preferred_element_type=F32).astype(BF).astype(F32)
    sigma = jax.nn.sigmoid(gates)
    active = gates * sigma
    slope = sigma * (1.0 + gates * (1.0 - sigma)) * values.astype(F32)

    def branch(incoming):
        mixed = jnp.dot(incoming, out_full.T, preferred_element_type=F32).astype(BF)
        mixed = mixed.reshape(blocks_dev, order, width)
        spread = lax.all_to_all(mixed, "seq", split_axis=1, concat_axis=0, tiled=True)
        part = spread.shape[1]
        left_part = jnp.dot(left_full.T, spread.reshape(blocks_all, part * width), preferred_element_type=F32).astype(BF)
        left_part = left_part.reshape(blocks_all, part, width)
        left_part = lax.all_to_all(left_part, "seq", split_axis=0, concat_axis=1, tiled=True)
        turned = (left_part.astype(F32) * twiddle_own[:, :, None]).astype(BF)
        right_part = jnp.einsum("pb,apc->abc", right_full, turned, preferred_element_type=F32).astype(BF)
        right_wide = right_part.reshape(tokens_dev, width).astype(F32)
        grad_value = (right_wide * active).astype(BF)
        grad_gate = (right_wide * slope).astype(BF)
        total = incoming.astype(F32)
        total = total + jnp.dot(grad_value, value_full.T, preferred_element_type=F32)
        total = total + jnp.dot(grad_gate, gate_full.T, preferred_element_type=F32)
        return total.astype(BF)

    first = branch(grad_out)
    second = branch(lax.ppermute(first, "pipe", [(1, 0)]))
    return jnp.where(lax.axis_index("pipe") == 1, first, second)[None]


def solution(mesh):
    fast = mesh.shape["pipe"] == 2 and mesh.shape["seq"] == SHARDS
    whole = P("pipe", "seq", None)
    in_specs = (whole, P("seq", None)) + (whole,) * 6
    return jax.shard_map(
        fast_body if fast else plain_body, mesh=mesh, in_specs=in_specs, out_specs=whole, check_vma=False
    )
```

```python
import jax
import jax.numpy as jnp
from jax import lax
from jax.experimental import pallas as pl
from jax.experimental.pallas import tpu as pltpu
from jax.sharding import PartitionSpec as P

BF = jnp.bfloat16
F32 = jnp.float32
SHARDS = 16
ANY = pl.BlockSpec(memory_space=pl.ANY)
VMEM = pl.BlockSpec(memory_space=pltpu.VMEM)
LIGHT = pl.CostEstimate(flops=1, bytes_accessed=1, transcendentals=0)
PARAMS = pltpu.CompilerParams(vmem_limit_bytes=62 * 1024 * 1024)

RIGHT, OUT, VALUE, GATE, ROWS = 0, 256, 400, 544, 688


def dot_nn(a, b):
    return lax.dot_general(a, b, (((1,), (0,)), ((), ())), preferred_element_type=F32)


def dot_nt(a, b):
    return lax.dot_general(a, b, (((1,), (1,)), ((), ())), preferred_element_type=F32)


def dot_tn(a, b):
    return lax.dot_general(a, b, (((0,), (0,)), ((), ())), preferred_element_type=F32)


def pack_kernel(right, out, value, gate, blob):
    for g in range(4):
        blob[RIGHT + 64 * g : RIGHT + 64 * g + 64, :] = right[0, :, 256 * g : 256 * g + 256]
    for base, ref in ((OUT, out), (VALUE, value), (GATE, gate)):
        for g in range(3):
            blob[base + 48 * g : base + 48 * g + 48, :] = ref[0, :, 256 * g : 256 * g + 256]


def pack(right, out, value, gate):
    return pl.pallas_call(
        pack_kernel,
        out_shape=jax.ShapeDtypeStruct((ROWS, 256), BF),
        in_specs=[VMEM] * 4,
        out_specs=VMEM,
        name="pack",
        cost_estimate=LIGHT,
    )(right, out, value, gate)


GROUPS = 25


def group_copies(block, out, sems, first, count):
    return [
        pltpu.make_async_copy(
            block.at[pl.ds(first, count), :, :, pl.ds(128 * c, 128)],
            out.at[pl.ds(first, count), pl.ds(4 * c, 4)],
            sems.at[c],
        )
        for c in range(6)
    ]


def factor_group(factor, tail, out, sem):
    tail[...] = jnp.zeros((SHARDS, 16, 128), BF)
    tail[:, :, 0:16] = jnp.broadcast_to(factor[0], (SHARDS, 16, 16))
    return pltpu.make_async_copy(tail, out.at[:, GROUPS - 1], sem)


def rows_kernel(section, source, factor, out, block, tail, sems):
    @pl.when(lax.axis_index("pipe") != section)
    def _():
        loads = [pltpu.make_async_copy(source.at[pl.ds(8 * t, 8)], block.at[pl.ds(8 * t, 8)], sems.at[t]) for t in range(2)]
        for c in loads:
            c.start()
        stores = [factor_group(factor, tail, out, sems.at[2])]
        stores[0].start()
        for t in range(2):
            loads[t].wait()
            copies = group_copies(block, out, sems.at[pl.ds(3 + 6 * t, 6)], 8 * t, 8)
            for c in copies:
                c.start()
            stores += copies
        for c in stores:
            c.wait()


def rows_to_send(section, source, factor):
    return pl.pallas_call(
        lambda *refs: rows_kernel(section, *refs),
        out_shape=jax.ShapeDtypeStruct((SHARDS, GROUPS, 16, 128), BF),
        in_specs=[ANY, VMEM],
        out_specs=ANY,
        scratch_shapes=[pltpu.VMEM((SHARDS, 4, 16, 768), BF), pltpu.VMEM((SHARDS, 16, 128), BF), pltpu.SemaphoreType.DMA((15,))],
        compiler_params=PARAMS,
        name="rows",
        cost_estimate=LIGHT,
    )(source.reshape(SHARDS, 4, 16, 768), factor)


def mix_kernel(left, x, y, matrix):
    @pl.when(pl.program_id(0) == 0)
    def _():
        rows = lax.broadcasted_iota(jnp.int32, (256, 16), 0)
        cols = lax.broadcasted_iota(jnp.int32, (256, 16), 1)
        spread = jnp.where(rows // 16 == cols, 1.0, 0.0).astype(BF)
        wide = dot_nt(dot_nt(spread, left[:, 0, 0, 0:16]).astype(BF), spread)
        at = lax.broadcasted_iota(jnp.int32, (256, 256), 0) % 16
        to = lax.broadcasted_iota(jnp.int32, (256, 256), 1) % 16
        matrix[...] = jnp.where(at == to, wide, 0.0).astype(BF)

    for q in range(4):
        part = jnp.concatenate([x[:, 4 * c + q, :, :].reshape(256, 128) for c in range(3)], axis=1)
        y[:, 16 * q : 16 * q + 16, :] = dot_nn(matrix[...], part).astype(BF).reshape(16, 16, 384)


def mix(x):
    return pl.pallas_call(
        mix_kernel,
        grid=(2,),
        out_shape=jax.ShapeDtypeStruct((SHARDS, 64, 768), BF),
        in_specs=[
            pl.BlockSpec((SHARDS, 1, 16, 128), lambda i: (0, GROUPS - 1, 0, 0)),
            pl.BlockSpec((SHARDS, 12, 16, 128), lambda i: (0, i, 0, 0)),
        ],
        out_specs=pl.BlockSpec((SHARDS, 64, 384), lambda i: (0, 0, i)),
        scratch_shapes=[pltpu.VMEM((256, 256), BF)],
        name="mix",
        cost_estimate=LIGHT,
    )(x, x)


def stack_kernel(section, n, *refs):
    ins, out, scratch, sems = refs[:n], refs[n], refs[n + 1], refs[n + 2]

    @pl.when(lax.axis_index("pipe") == section)
    def _():
        copies = [pltpu.make_async_copy(r, scratch.at[pl.ds(ROWS * i, ROWS), :], sems.at[i]) for i, r in enumerate(ins)]
        stores = [
            pltpu.make_async_copy(scratch.at[pl.ds(ROWS * i, ROWS), :], out.at[pl.ds(ROWS * i, ROWS), :], sems.at[n + i])
            for i in range(n)
        ]
        for c in copies:
            c.start()
        for c, d in zip(copies, stores):
            c.wait()
            d.start()
        for d in stores:
            d.wait()


def stacked(section, *parts):
    n = len(parts)
    return pl.pallas_call(
        lambda *refs: stack_kernel(section, n, *refs),
        out_shape=jax.ShapeDtypeStruct((ROWS * n, 256), BF),
        in_specs=[ANY] * n,
        out_specs=ANY,
        scratch_shapes=[pltpu.VMEM((ROWS * n, 256), BF), pltpu.SemaphoreType.DMA((2 * n,))],
        compiler_params=PARAMS,
        name="stack",
        cost_estimate=LIGHT,
    )(*parts)


def weight_copies(pieces, refs, scratch, sems, first, count):
    seq = lax.axis_index("seq")
    z, place = seq // 4, seq % 4
    copies = []
    for (at, shift, step, offset), ref in zip(pieces, refs):
        del at
        for n, k in enumerate(shift):
            shard = lax.rem(z - k + 4, 4) * 4 + jnp.bitwise_xor(place, step)
            copies.append(
                pltpu.make_async_copy(
                    ref.at[pl.ds(offset + n * ROWS + first, count), :],
                    scratch.at[shard, pl.ds(first, count), :],
                    sems.at[len(copies)],
                )
            )
    assert len(copies) == SHARDS
    return copies


def lanes_of(scratch, base, rows, groups):
    parts = [scratch[:, base + rows * g : base + rows * g + rows, :].reshape(SHARDS * rows, 256) for g in range(groups)]
    return jnp.concatenate(parts, axis=1)


def forward_work(pieces, n_refs, *refs):
    x, twiddle, weights, refs = refs[0], refs[1], refs[2 : 2 + n_refs], refs[2 + n_refs :]
    active, slope, turning, gathered, scratch, rows_in, act, slo, right, sem_w, sem, sem_out = refs
    tiles = [slice(256 * t, 256 * t + 256) for t in range(4)]
    loads = [pltpu.make_async_copy(x.at[0, rows], rows_in.at[rows], sem.at[t]) for t, rows in enumerate(tiles)]
    copies = weight_copies(pieces, weights, scratch, sem_w, 0, ROWS)
    for c in loads[:1] + copies + loads[1:]:
        c.start()
    for c in copies:
        c.wait()
    stores = []

    def store(source, target):
        stores.append(pltpu.make_async_copy(source, target, sem_out.at[len(stores)]))
        stores[-1].start()

    store(scratch.at[:, pl.ds(OUT, ROWS - OUT), :], gathered)
    for t, rows in enumerate(tiles):
        loads[t].wait()
        part = scratch[:, RIGHT + 64 * t : RIGHT + 64 * t + 64, :].reshape(1024, 256)
        right[rows, :] = (part.T.astype(F32) * twiddle[...]).astype(BF)
        store(right.at[rows], turning.at[rows])
        for e in range(3):
            lanes = slice(256 * e, 256 * e + 256)
            value = scratch[:, VALUE + 48 * e : VALUE + 48 * e + 48, :].reshape(768, 256)
            gate = scratch[:, GATE + 48 * e : GATE + 48 * e + 48, :].reshape(768, 256)
            values = dot_nn(rows_in[rows, :], value).astype(BF).astype(F32)
            gates = dot_nn(rows_in[rows, :], gate).astype(BF).astype(F32)
            sigma = 0.5 + 0.5 * jnp.tanh(0.5 * gates)
            on = gates * sigma
            act[rows, lanes] = on.astype(BF)
            slo[rows, lanes] = ((sigma + on * (1.0 - sigma)) * values).astype(BF)
        store(act.at[rows], active.at[rows])
        store(slo.at[rows], slope.at[rows])
    for c in stores:
        c.wait()


def forward_kernel(section, pieces, n_refs, *refs):
    @pl.when(lax.axis_index("pipe") == section)
    def _():
        forward_work(pieces, n_refs, *refs)


def forward(section, x, twiddle, pieces, weights):
    shape = jax.ShapeDtypeStruct((1024, 768), BF)
    square = jax.ShapeDtypeStruct((1024, 1024), BF)
    rows = jax.ShapeDtypeStruct((SHARDS, ROWS - OUT, 256), BF)
    big = pltpu.VMEM((1024, 768), BF)
    return pl.pallas_call(
        lambda *refs: forward_kernel(section, pieces, len(weights), *refs),
        out_shape=(shape, shape, square, rows),
        in_specs=[ANY, VMEM] + [ANY] * len(weights),
        out_specs=(ANY,) * 4,
        scratch_shapes=[pltpu.VMEM((SHARDS, ROWS, 256), BF), big, big, big, pltpu.VMEM((1024, 1024), BF)]
        + [pltpu.SemaphoreType.DMA((SHARDS,)), pltpu.SemaphoreType.DMA((4,)), pltpu.SemaphoreType.DMA((13,))],
        compiler_params=PARAMS,
        name="forward",
        cost_estimate=LIGHT,
    )(x, twiddle, *weights)


def layer_work(last, *refs):
    given, active, slope, turning, gathered, incoming = refs[:6]
    if last:
        result, refs = refs[7], refs[8:]
    else:
        factor, result, out, refs = refs[6], refs[7], refs[8], refs[9:]
    weights, left, right, inner, act, slo, base, total, sem, sem_out, *tail = refs
    halves = (slice(0, 512), slice(512, 1024))
    loads = []

    def load(source, target):
        loads.append(pltpu.make_async_copy(source, target, sem.at[len(loads)]))
        loads[-1].start()
        return loads[-1]

    part = load(given, left)
    rights = [load(turning.at[h], right.at[h]) for h in halves]
    projections = load(gathered, weights)
    gates = []
    for h in halves:
        gates += [load(active.at[h], act.at[h]), load(slope.at[h], slo.at[h]), load(incoming.at[h], base.at[h])]
    part.wait()
    for c, h in zip(rights, halves):
        c.wait()
        inner[h, :] = dot_nn(right[h, :], left[...]).astype(BF)
    projections.wait()
    stores = [] if last else [factor_group(factor, tail[0], out, sem_out.at[4])]
    for c in stores:
        c.start()
    for t in range(4):
        rows = slice(256 * t, 256 * t + 256)
        pieces = slice(4 * t, 4 * t + 4)
        right_part = dot_nt(inner[rows, :], lanes_of(weights, 0, 48, 3)).astype(BF).astype(F32)
        if t % 2 == 0:
            for c in gates[3 * (t // 2) : 3 * (t // 2) + 3]:
                c.wait()
        grad_value = (right_part * act[rows, :].astype(F32)).astype(BF)
        grad_gate = (right_part * slo[rows, :].astype(F32)).astype(BF)
        added = dot_nt(grad_value, lanes_of(weights, VALUE - OUT, 48, 3)) + dot_nt(grad_gate, lanes_of(weights, GATE - OUT, 48, 3))
        total[pieces] = (base[rows, :].astype(F32) + added).astype(BF).reshape(4, 4, 16, 768)
        copies = [pltpu.make_async_copy(total.at[pieces], result.at[pieces], sem_out.at[t])]
        if not last:
            copies += group_copies(total, out, sem_out.at[pl.ds(5 + 6 * t, 6)], 4 * t, 4)
        for c in copies:
            c.start()
        stores += copies
    for c in stores:
        c.wait()


def layer_kernel(section, last, *refs):
    pipe = lax.axis_index("pipe")

    @pl.when(pipe == section)
    def _():
        layer_work(last, *refs)

    if last:

        @pl.when(pipe != section)
        def _():
            own, result = refs[6], refs[7]
            total, sem, sem_out = refs[-3:]
            halves = [pl.ds(8 * t, 8) for t in range(2)]
            loads = [pltpu.make_async_copy(own.at[h], total.at[h], sem.at[t]) for t, h in enumerate(halves)]
            stores = [pltpu.make_async_copy(total.at[h], result.at[h], sem_out.at[t]) for t, h in enumerate(halves)]
            for c in loads:
                c.start()
            for load, store in zip(loads, stores):
                load.wait()
                store.start()
            for c in stores:
                c.wait()


def layer(section, left, gated, incoming, other, last):
    whole = jax.ShapeDtypeStruct((SHARDS, 4, 16, 768), BF)
    groups = jax.ShapeDtypeStruct((SHARDS, GROUPS, 16, 128), BF)
    big = pltpu.VMEM((1024, 768), BF)
    return pl.pallas_call(
        lambda *refs: layer_kernel(section, last, *refs),
        out_shape=whole if last else (whole, groups),
        in_specs=[ANY] * (2 + len(gated)) + [ANY if last else VMEM],
        out_specs=ANY if last else (ANY, ANY),
        scratch_shapes=[pltpu.VMEM((SHARDS, ROWS - OUT, 256), BF), big, pltpu.VMEM((1024, 1024), BF)]
        + [big] * 4
        + [pltpu.VMEM((SHARDS, 4, 16, 768), BF), pltpu.SemaphoreType.DMA((10,)), pltpu.SemaphoreType.DMA((29,))]
        + ([] if last else [pltpu.VMEM((SHARDS, 16, 128), BF)]),
        compiler_params=PARAMS,
        name="layer",
        cost_estimate=LIGHT,
    )(left, *gated, incoming, other)


def sent(x, section, to):
    pairs = [(section * SHARDS + s, section * SHARDS + to(s)) for s in range(SHARDS)]
    return lax.ppermute(x, ("pipe", "seq"), pairs)


def along_z(x, section, k):
    return sent(x, section, lambda s: ((s // 4 + k) % 4) * 4 + s % 4)


def in_plane(x, section, d):
    return sent(x, section, lambda s: s ^ d)


def exchanged(x):
    return lax.all_to_all(x, "seq", split_axis=0, concat_axis=0, tiled=True)


def tied(*xs):
    return lax.optimization_barrier(xs)


PIECES = (
    [(0, (0,), 0, 0)]
    + [(0, (k,), 0, 0) for k in (1, 2, 3)]
    + [(0, (0,), d, 0) for d in (3, 1, 2)]
    + [(0, (1, 2, 3), d, 0) for d in (3, 1, 2)]
)


def only_on(core, f, *args):
    shapes, tree = jax.tree.flatten(jax.eval_shape(f, *args))

    def idle(*_):
        arrays = pl.pallas_call(
            lambda *refs: None, out_shape=shapes, out_specs=[ANY] * len(shapes), name="idle", cost_estimate=LIGHT
        )()
        return jax.tree.unflatten(tree, arrays)

    return lax.cond(lax.axis_index("pipe") == core, f, idle, *args)


def mixed(rows):
    return exchanged(mix(exchanged(rows))).reshape(1024, 768)


def fast_body(inputs_saved, grad_out, value_weight, gate_weight, out_weight, right_factor, left_factor, twiddle):
    got_left = lax.ppermute(left_factor, "pipe", [(0, 1), (1, 0)])
    blob, got_left = tied(pack(right_factor, out_weight, value_weight, gate_weight), got_left)

    along = [along_z(blob, 1, k) for k in (1, 2, 3)]
    own = [in_plane(blob, 1, d) for d in (3, 1, 2)]
    rest, *own = tied(stacked(1, *along), *own)
    plane = [in_plane(rest, 1, d) for d in (3, 1, 2)]
    left = only_on(0, mixed, rows_to_send(1, grad_out, got_left))
    left, *plane = tied(left, *plane)
    gated = forward(1, inputs_saved, twiddle[0], PIECES, [blob, *along, *own, *plane])
    left, later_blob, *gated = tied(left, blob, *gated)
    got = lax.ppermute(left, "pipe", [(0, 1)])
    along = [along_z(later_blob, 0, k) for k in (1, 2, 3)]
    own = [in_plane(later_blob, 0, d) for d in (3, 1, 2)]
    grad, rows = layer(1, got, gated, grad_out, got_left, False)
    grad, rows, *moved = tied(grad, rows, *along, *own)
    along, own = moved[:3], moved[3:]

    got_grad = lax.ppermute(grad.reshape(1024, 768), "pipe", [(1, 0)])
    left, later_blob, *moved = tied(only_on(1, mixed, rows), later_blob, *along, *own)
    got = lax.ppermute(left, "pipe", [(1, 0)])

    def gathered(x, twiddle, blob, *moved):
        rest = stacked(0, *moved[:3])
        plane = [in_plane(rest, 0, d) for d in (3, 1, 2)]
        return forward(0, x, twiddle, PIECES, [blob, *moved, *plane])

    gated = only_on(0, gathered, inputs_saved, twiddle[0], later_blob, *moved)
    return layer(0, got, gated, got_grad, grad, True).reshape(1, 1024, 768)


def plain_body(inputs_saved, grad_out, value_weight, gate_weight, out_weight, right_factor, left_factor, twiddle):
    value_full, gate_full, out_full, right_full, left_full = (
        lax.all_gather(w[0], "seq", axis=0, tiled=True)
        for w in (value_weight, gate_weight, out_weight, right_factor, left_factor)
    )
    twiddle_own = twiddle[0]
    saved = inputs_saved[0]
    tokens_dev, width = saved.shape
    order = right_full.shape[0]
    blocks_dev, blocks_all = tokens_dev // order, left_full.shape[0]
    values = jnp.dot(saved, value_full, preferred_element_type=F32).astype(BF)
    gates = jnp.dot(saved, gate_full, preferred_element_type=F32).astype(BF).astype(F32)
    sigma = jax.nn.sigmoid(gates)
    active = gates * sigma
    slope = sigma * (1.0 + gates * (1.0 - sigma)) * values.astype(F32)

    def branch(incoming):
        mixed = jnp.dot(incoming, out_full.T, preferred_element_type=F32).astype(BF)
        mixed = mixed.reshape(blocks_dev, order, width)
        spread = lax.all_to_all(mixed, "seq", split_axis=1, concat_axis=0, tiled=True)
        part = spread.shape[1]
        left_part = jnp.dot(left_full.T, spread.reshape(blocks_all, part * width), preferred_element_type=F32).astype(BF)
        left_part = left_part.reshape(blocks_all, part, width)
        left_part = lax.all_to_all(left_part, "seq", split_axis=0, concat_axis=1, tiled=True)
        turned = (left_part.astype(F32) * twiddle_own[:, :, None]).astype(BF)
        right_part = jnp.einsum("pb,apc->abc", right_full, turned, preferred_element_type=F32).astype(BF)
        right_wide = right_part.reshape(tokens_dev, width).astype(F32)
        grad_value = (right_wide * active).astype(BF)
        grad_gate = (right_wide * slope).astype(BF)
        total = incoming.astype(F32)
        total = total + jnp.dot(grad_value, value_full.T, preferred_element_type=F32)
        total = total + jnp.dot(grad_gate, gate_full.T, preferred_element_type=F32)
        return total.astype(BF)

    first = branch(grad_out)
    second = branch(lax.ppermute(first, "pipe", [(1, 0)]))
    return jnp.where(lax.axis_index("pipe") == 1, first, second)[None]


def solution(mesh):
    fast = mesh.shape["pipe"] == 2 and mesh.shape["seq"] == SHARDS
    whole = P("pipe", "seq", None)
    in_specs = (whole, P("seq", None)) + (whole,) * 6
    return jax.shard_map(
        fast_body if fast else plain_body, mesh=mesh, in_specs=in_specs, out_specs=whole, check_vma=False
    )
```
